256 devices in a mesh: tile: 32 (over x, z_lo, core), var: 8 (over y, z_hi).
Axes of the slice: x: 4, y: 4, z: 8 (z_hi: 2, z_lo: 4; z = z_hi * 4 + z_lo), core: 2. Of those that a mesh axis runs over, the one named last changes fastest.
Arguments:
- range_sq: float32 [8, 512, 2048], P('var', 'tile'), may hold values from 0.05 to 4
- state_field: float32 [8, 512, 2048], P('var', 'tile'), may hold values from -6 to 6
- coupling: float32 [8, 8], replicated, may hold values from -2 to 2
- obs_cell: int32 [131072], P('tile'), may hold values from 0 to 32767
- obs_value: float32 [8, 131072], P('var', 'tile'), may hold values from -6 to 6
Outputs:
- adjoint: float32 [8, 512, 2048], P('var', 'tile')
- range_grad: float32 [8, 512, 2048], P('var', 'tile')
The draws below stay inside these ranges and needn't reach their ends.
Inputs may be any that keep to these rules, and one draw needn't show every extreme that they name: `obs_cell`: each strip's 4096 entries index cells of that strip; cells may repeat.
All inputs are finite; a program needn't handle non-finite values.
Results may differ from the reference program's by a relative error of at most 0.00017.
Values sent between devices are 32-bit elements; how exact they have to be, the bound alone decides.
No kernel may reach another device: no remote copies, remote signals or barrier semaphores. Data moves between devices by JAX's collectives and lax.ppermute only.
A program may use at most 64 MiB of HBM per device.

```python
import math
import jax
import jax.numpy as jnp
from jax import lax

ROWS_DEV = 16
COLS = 2048
ITERS = 4
VARS = 8
ROWS = 512
OBS_DEV = 4096
OBS = 131072


def set_ends(drawn, rng, smallest, top_value):
    longest = drawn.shape.index(max(drawn.shape))
    spots = []
    for shift in (0, 1):
        where = [jax.random.randint(jax.random.fold_in(rng, axis), (), 0, length) for axis, length in enumerate(drawn.shape)]
        where[longest] = (where[longest] + shift) % drawn.shape[longest]
        spots.append(tuple(where))
    return drawn.at[spots[0]].set(smallest).at[spots[1]].set(top_value)


def levels(own_key, shape, pieces, least, top_value):
    level, own = 1.0, jax.random.fold_in(own_key, 6)
    for dim, parts in pieces:
        steps = jnp.exp(jax.random.uniform(jax.random.fold_in(own, dim), (parts,), jnp.float32, least / len(pieces), top_value / len(pieces)))
        level = level * jnp.repeat(steps, shape[dim] // parts).reshape([-1 if axis == dim else 1 for axis in range(len(shape))])
    return level


def scatter_about(key, shape, spread, bound, cuts=(), held_as=jnp.bfloat16):
    values = jax.random.normal(key, shape, jnp.float32) * spread
    if len(cuts) > 0:
        values = levels(key, shape, cuts, -0.22, 0.18) * values
    return jnp.clip(values, min=-bound, max=bound).astype(held_as)


def setup_inputs(seed: int = 0) -> dict:
    streams_of = jax.random.split(jax.random.key(seed), 6)
    range_sq = jnp.clip(jnp.exp(math.log(4.0) - 4.3820266 * jax.random.uniform(streams_of[0], (VARS, ROWS, COLS), jnp.float32) ** levels(streams_of[0], (VARS, ROWS, COLS), ((0, 8), (1, 32)), -0.2, 0.2)), 0.05, 4.0)
    state_field = scatter_about(streams_of[1], (VARS, ROWS, COLS), 1.0, 6.0, ((0, 8), (1, 32)), jnp.float32)
    coupling = scatter_about(streams_of[2], (VARS, VARS), (0.4 / VARS ** 0.5), 2.0, (), jnp.float32)
    obs_cell = set_ends(jax.random.randint(streams_of[3], (OBS,), 0, ROWS_DEV * COLS), jax.random.fold_in(streams_of[3], 1), 0, (ROWS_DEV * COLS) - 1).astype(jnp.int32)
    obs_value = scatter_about(streams_of[4], (VARS, OBS), 1.0, 6.0, ((0, 8), (1, 32)), jnp.float32)
    return dict(range_sq=range_sq, state_field=state_field, coupling=coupling, obs_cell=obs_cell, obs_value=obs_value)


def shape_op(field, kappa):
    padded = jnp.pad(field, ((0, 0), (1, 1), (1, 1)))
    beside = padded[:, 2:, 1:-1] + padded[:, :-2, 1:-1] + padded[:, 1:-1, 2:] + padded[:, 1:-1, :-2]
    return ((kappa + 4.0) * field - beside) * 0.125


def couple(mixing, field):
    mixed = jnp.einsum("vw,wrc->vrc", mixing, field, precision=lax.Precision.HIGHEST)
    return jnp.einsum("wv,wrc->vrc", mixing, mixed, precision=lax.Precision.HIGHEST)


def reference(range_sq, state_field, coupling, obs_cell, obs_value):
    mixing = jnp.eye(VARS, dtype=jnp.float32) + coupling
    entries = obs_cell.shape[0]
    owner = jnp.arange(entries, dtype=jnp.int32) // OBS_DEV
    flat = owner * (ROWS_DEV * COLS) + obs_cell
    source = jnp.zeros((VARS, ROWS * COLS), jnp.float32).at[:, flat].add(obs_value)
    source = source.reshape(VARS, ROWS, COLS)
    theta = 4.025
    delta = 3.975
    sigma = theta / delta
    adjoint = jnp.zeros_like(source)
    resid = source
    rho = 1.0 / sigma
    direction = resid / theta
    for step in range(ITERS):
        adjoint = adjoint + direction
        if step < ITERS - 1:
            resid = resid - shape_op(couple(mixing, shape_op(direction, range_sq)), range_sq)
            rho_new = 1.0 / (2.0 * sigma - rho)
            direction = rho_new * rho * direction + (2.0 * rho_new / delta) * resid
            rho = rho_new
    first = couple(mixing, shape_op(adjoint, range_sq)) * state_field
    second = adjoint * couple(mixing, shape_op(state_field, range_sq))
    range_grad = -(first + second) * 0.125
    return adjoint, range_grad
```

```python
import functools

import jax
import jax.numpy as jnp
from jax import lax
from jax.experimental import pallas as pl
from jax.experimental.pallas import tpu as pltpu
from jax.sharding import PartitionSpec as P

ITERS = 4
THETA = 4.025
DELTA = 3.975
VMEM = pl.BlockSpec(memory_space=pltpu.VMEM)
SMEM = pl.BlockSpec(memory_space=pltpu.SMEM)

ROWS, COLS, VARS, GROUPS = 16, 2048, 8, 4
BLOCK = COLS // GROUPS
SIDE = 128
WIDE = BLOCK + SIDE
EDGE = 8
TALL = ROWS + 2 * EDGE
OBS = 4096
OBS_ROWS = OBS // BLOCK


def group_place():
    var = lax.axis_index("var")
    return var // 2, lax.rem(var, 2)


def window(ref, block, rows):
    main = ref[:, pl.ds(pl.multiple_of(block * BLOCK, BLOCK), BLOCK)]
    after = jnp.minimum(block + 1, GROUPS - 1) * BLOCK
    before = jnp.maximum(block * BLOCK - SIDE, 0)
    right = ref[:, pl.ds(pl.multiple_of(after, SIDE), SIDE)]
    left = ref[:, pl.ds(pl.multiple_of(before, SIDE), SIDE)]
    lane = lax.broadcasted_iota(jnp.int32, (rows, SIDE), 1)
    return main, jnp.where(lane < SIDE // 2, right, left)


def pack_state_kernel(state_ref, *outs):
    y, _ = group_place()
    for k in range(GROUPS):
        main, side = window(state_ref, lax.rem(y + k, GROUPS), ROWS)
        outs[k][:, :BLOCK] = main
        outs[k][:, BLOCK:] = side


def pack_kappa_kernel(own_ref, other_ref, own_obs_ref, other_obs_ref, *outs):
    y, _ = group_place()
    for k in range(GROUPS):
        for slot, (ref, obs) in enumerate(((own_ref, own_obs_ref), (other_ref, other_obs_ref))):
            main, side = window(ref, lax.rem(y + k, GROUPS), ROWS)
            outs[k][slot, :ROWS, :BLOCK] = main
            outs[k][slot, :ROWS, BLOCK:] = side
            for i in range(OBS_ROWS):
                outs[k][slot, ROWS + i : ROWS + i + 1, :BLOCK] = obs[:, i * BLOCK : (i + 1) * BLOCK]


def scatter_kernel(cell_ref, k0, k1, k2, k3, sa_ref, sb_ref, source_ref, up_ref, down_ref, acc):
    y, z = group_place()
    pieces = (k0, k1, k2, k3)
    acc[...] = jnp.zeros_like(acc)
    rows = lax.broadcasted_iota(jnp.int32, (ROWS, BLOCK), 0)
    lanes = lax.broadcasted_iota(jnp.int32, (WIDE, BLOCK), 0)
    half = SIDE // 2
    for i in range(OBS_ROWS):
        cell = cell_ref[:, i * BLOCK : (i + 1) * BLOCK]
        row = lax.shift_right_logical(cell, 11)
        col = jnp.bitwise_and(cell, COLS - 1) - y * BLOCK
        place = jnp.where(
            (col >= 0) & (col < BLOCK + half), col, jnp.where((col >= -half) & (col < 0), col + WIDE, -1)
        )
        hit_row = rows == row
        hit_col = jnp.where(lanes == place, 1.0, 0.0).astype(jnp.bfloat16)
        highs, lows = [], []
        for k in range(GROUPS):
            for slot in range(2):
                value = pieces[k][slot, ROWS + i : ROWS + i + 1, :BLOCK]
                high = value.astype(jnp.bfloat16).astype(jnp.float32)
                low = value - high
                highs.append(jnp.where(hit_row, high, 0.0).astype(jnp.bfloat16))
                lows.append(jnp.where(hit_row, low, 0.0).astype(jnp.bfloat16))
        values = jnp.concatenate(highs + lows, axis=0)
        acc[...] += lax.dot_general(
            values, hit_col, (((1,), (1,)), ((), ())), preferred_element_type=jnp.float32
        )
    count = VARS * ROWS
    for k in range(GROUPS):
        for slot in range(2):
            at = (k * 2 + slot) * ROWS
            total = acc[at : at + ROWS] + acc[count + at : count + at + ROWS]
            var = 2 * lax.rem(y - k + GROUPS, GROUPS) + lax.rem(z + slot, 2)
            source_ref[var] = total
            up_ref[0, var] = total[:EDGE]
            down_ref[0, var] = total[EDGE:]
            kappa = pieces[k][slot, :ROWS]
            up_ref[1, var] = kappa[:EDGE]
            down_ref[1, var] = kappa[EDGE:]
            state = (sa_ref, sb_ref)[slot]
            up_ref[2, 0, pl.ds(var, 1), :] = state[k, 0:1, :]
            down_ref[2, 0, pl.ds(var, 1), :] = state[k, ROWS - 1 : ROWS, :]


def shape_rows(u):
    return pltpu.roll(u, 1, 0) + pltpu.roll(u, TALL - 1, 0) + pltpu.roll(u, 1, 1) + pltpu.roll(u, WIDE - 1, 1)


def main_kernel(
    mix_ref, source_ref, above_ref, below_ref, k0, k1, k2, k3, sa_ref, sb_ref, o0, o1, o2, o3,
    kp, adj, res, dirn, tmp, state, mask_ref
):
    y, z = group_place()
    tile = lax.axis_index("tile")
    pieces = (k0, k1, k2, k3)
    row = lax.broadcasted_iota(jnp.int32, (TALL, WIDE), 0)
    lane = lax.broadcasted_iota(jnp.int32, (TALL, WIDE), 1)
    row = jnp.where(row < ROWS + EDGE, row, row - TALL) + tile * ROWS
    lane = jnp.where(lane < BLOCK + SIDE // 2, lane, lane - WIDE) + y * BLOCK
    inside = (row >= 0) & (row < ROWS * lax.axis_size("tile")) & (lane >= 0) & (lane < COLS)
    mask_ref[...] = jnp.where(inside, 1.0, 0.0)
    mask = mask_ref[...]
    for k in range(GROUPS):
        for slot in range(2):
            var = 2 * lax.rem(y - k + GROUPS, GROUPS) + lax.rem(z + slot, 2)
            kp[var, :ROWS] = pieces[k][slot, :ROWS] + 4.0
            state[var, :ROWS] = (sa_ref, sb_ref)[slot][k]
    kp[:, ROWS : ROWS + EDGE] = below_ref[1] + 4.0
    kp[:, ROWS + EDGE :] = above_ref[1] + 4.0
    for var in range(VARS):
        state[var, ROWS : ROWS + 1] = below_ref[2, 0, var : var + 1, :]
        state[var, ROWS + 1 : TALL - 1] = jnp.zeros((TALL - ROWS - 2, WIDE), jnp.float32)
        state[var, TALL - 1 :] = above_ref[2, 0, var : var + 1, :]

    def fill(var, _):
        kp[var] = kp[var] * mask_ref[...]
        state[var] = state[var] * mask_ref[...]
        for at, part in ((0, source_ref[var]), (ROWS, below_ref[0, var]), (ROWS + EDGE, above_ref[0, var])):
            part = part * mask_ref[at : at + part.shape[0]]
            res[var, at : at + part.shape[0]] = part
            part = part * (1.0 / THETA)
            dirn[var, at : at + part.shape[0]] = part
            adj[var, at : at + part.shape[0]] = part
        return 0

    lax.fori_loop(0, VARS, fill, 0)

    def shape(src, var):
        u = src[var]
        return kp[var] * u - shape_rows(u) * mask_ref[...]

    def couple(ref):
        def step(at, _):
            at = pl.multiple_of(at * 8, 8)
            for c in range(WIDE // 128):
                cols = slice(c * 128, (c + 1) * 128)
                fields = [ref[w, pl.ds(at, 8), cols] for w in range(VARS)]
                for v in range(VARS):
                    total = mix_ref[v, 0] * fields[0]
                    for w in range(1, VARS):
                        total = total + mix_ref[v, w] * fields[w]
                    ref[v, pl.ds(at, 8), cols] = total
            return 0

        lax.fori_loop(0, TALL // 8, step, 0)

    sigma = THETA / DELTA
    rho = 1.0 / sigma
    for _ in range(ITERS - 1):
        rho_new = 1.0 / (2.0 * sigma - rho)
        c1, c2 = rho_new * rho, 2.0 * rho_new / DELTA
        rho = rho_new

        def first(var, _):
            tmp[var] = shape(dirn, var)
            return 0

        lax.fori_loop(0, VARS, first, 0)
        couple(tmp)

        def second(var, _):
            r = res[var] - shape(tmp, var)
            res[var] = r
            d = c1 * dirn[var] + c2 * r
            dirn[var] = d
            adj[var] = adj[var] + d
            return 0

        lax.fori_loop(0, VARS, second, 0)

    def last(var, _):
        tmp[var] = shape(adj, var)
        res[var] = shape(state, var)
        return 0

    lax.fori_loop(0, VARS, last, 0)
    for k, out in enumerate((o0, o1, o2, o3)):
        v = 2 * lax.rem(y + k, GROUPS) + z
        for r in range(0, ROWS, 8):
            for c in range(0, BLOCK, 128):
                here = (slice(r, r + 8), slice(c, c + 128))
                first_sum = mix_ref[v, 0] * tmp[(0,) + here]
                second_sum = mix_ref[v, 0] * res[(0,) + here]
                for w in range(1, VARS):
                    first_sum = first_sum + mix_ref[v, w] * tmp[(w,) + here]
                    second_sum = second_sum + mix_ref[v, w] * res[(w,) + here]
                a = adj[v, r : r + 8, c : c + 128]
                out[(0,) + here] = a
                out[(1,) + here] = -(first_sum * state[v, r : r + 8, c : c + 128] + a * second_sum)


def join_kernel(p0, p1, p2, p3, adjoint_ref, grad_ref):
    y, _ = group_place()
    for k, part in enumerate((p0, p1, p2, p3)):
        at = pl.multiple_of(lax.rem(y - k + GROUPS, GROUPS) * BLOCK, BLOCK)
        adjoint_ref[:, pl.ds(at, BLOCK)] = part[0]
        grad_ref[:, pl.ds(at, BLOCK)] = part[1]


def call(kernel, outs, n_in, smem=0, scratch=(), flops=1000, size=100000):
    shapes = [jax.ShapeDtypeStruct(s, jnp.float32) for s in outs]
    return pl.pallas_call(
        kernel,
        out_shape=shapes,
        in_specs=[SMEM] * smem + [VMEM] * (n_in - smem),
        out_specs=[VMEM] * len(shapes),
        scratch_shapes=list(scratch),
        compiler_params=pltpu.CompilerParams(vmem_limit_bytes=32 * 1024 * 1024),
        cost_estimate=pl.CostEstimate(flops=flops, bytes_accessed=size, transcendentals=0),
    )


def across(x):
    return lax.ppermute(x, "var", [(i, i ^ 1) for i in range(VARS)])


def around(x, k):
    return lax.ppermute(x, "var", [(i, (i // 2 + k) % GROUPS * 2 + i % 2) for i in range(VARS)])


def along(x, tiles, forward):
    pairs = []
    for i in range(tiles - 1):
        for v in range(VARS):
            ahead = (i + 1) * VARS + (v ^ 1 if i % 8 == 7 else v)
            pairs.append((i * VARS + v, ahead) if forward else (ahead, i * VARS + v))
    return lax.ppermute(x, ("tile", "var"), pairs)


def per_device(tiles, range_sq, state_field, coupling, obs_cell, obs_value):
    mixing = jnp.eye(VARS, dtype=jnp.float32) + coupling
    mix = jnp.einsum("uv,uw->vw", mixing, mixing, precision=lax.Precision.HIGHEST) * (1.0 / 64.0)
    kappa = range_sq[0]
    other_kappa = across(kappa)
    other_obs = across(obs_value)
    s0, s1, s2, s3 = call(pack_state_kernel, [(ROWS, WIDE)] * 4, 1)(state_field[0])
    states = jnp.stack([s0, around(s1, 1), around(s2, 2), around(s3, 3)])
    other_states = across(states)
    k0, k1, k2, k3 = call(pack_kappa_kernel, [(2, ROWS + OBS_ROWS, WIDE)] * 4, 4)(kappa, other_kappa, obs_value, other_obs)
    k1, k2, k3 = around(k1, 1), around(k2, 2), around(k3, 3)
    pieces = (k0, k1, k2, k3)
    source, up, down = call(
        scatter_kernel,
        [(VARS, ROWS, WIDE), (3, VARS, EDGE, WIDE), (3, VARS, EDGE, WIDE)],
        7,
        scratch=[pltpu.VMEM((2 * VARS * ROWS, WIDE), jnp.float32)],
    )(obs_cell.reshape(1, OBS), *pieces, states, other_states)
    above = along(down, tiles, True)
    below = along(up, tiles, False)
    field = pltpu.VMEM((VARS, TALL, WIDE), jnp.float32)
    parts = call(
        main_kernel,
        [(2, ROWS, BLOCK)] * 4,
        10,
        smem=1,
        scratch=[field] * 6 + [pltpu.VMEM((TALL, WIDE), jnp.float32)],
    )(mix, source, above, below, *pieces, states, other_states)
    parts = [parts[0]] + [around(parts[k], k) for k in range(1, GROUPS)]
    adjoint, grad = call(join_kernel, [(ROWS, COLS)] * 2, 4)(*parts)
    return adjoint[None], grad[None]


def solution(mesh):
    return jax.shard_map(
        functools.partial(per_device, mesh.shape["tile"]),
        mesh=mesh,
        in_specs=(P("var", "tile", None), P("var", "tile", None), P(), P("tile"), P("var", "tile")),
        out_specs=(P("var", "tile", None), P("var", "tile", None)),
        check_vma=False,
    )
```

```python
import functools

import jax
import jax.numpy as jnp
from jax import lax
from jax.experimental import pallas as pl
from jax.experimental.pallas import tpu as pltpu
from jax.sharding import PartitionSpec as P

ITERS = 4
THETA = 4.025
DELTA = 3.975
VMEM = pl.BlockSpec(memory_space=pltpu.VMEM)
SMEM = pl.BlockSpec(memory_space=pltpu.SMEM)

ROWS, COLS, VARS, GROUPS = 16, 2048, 8, 4
BLOCK = COLS // GROUPS
SIDE = 128
WIDE = BLOCK + SIDE
EDGE = 8
TALL = ROWS + 2 * EDGE
OBS = 4096
OBS_ROWS = OBS // BLOCK


def group_place():
    var = lax.axis_index("var")
    return var // 2, lax.rem(var, 2)


def ahead(y, k):
    return lax.rem(y + k, GROUPS)


def behind(y, k):
    return lax.rem(y - k + GROUPS, GROUPS)


def window(ref, block, rows):
    main = ref[rows, pl.ds(pl.multiple_of(block * BLOCK, BLOCK), BLOCK)]
    after = jnp.minimum(block + 1, GROUPS - 1) * BLOCK
    before = jnp.maximum(block * BLOCK - SIDE, 0)
    right = ref[rows, pl.ds(pl.multiple_of(after, SIDE), SIDE)]
    left = ref[rows, pl.ds(pl.multiple_of(before, SIDE), SIDE)]
    lane = lax.broadcasted_iota(jnp.int32, (8, SIDE), 1)
    return main, jnp.where(lane < SIDE // 2, right, left)


def extra_kernel(obs_ref, state_ref, extra_ref):
    for i in range(OBS_ROWS):
        extra_ref[i : i + 1, :BLOCK] = obs_ref[:, i * BLOCK : (i + 1) * BLOCK]
    for e, r in enumerate((0, ROWS - 1)):
        for block in range(GROUPS):
            for i in range(BLOCK // SIDE):
                to, at = e * (BLOCK // SIDE) + i, BLOCK + block * SIDE
                col = block * BLOCK + i * SIDE
                extra_ref[to : to + 1, at : at + SIDE] = state_ref[r : r + 1, col : col + SIDE]


def shape_kernel(kappa_ref, state_ref, shaped_ref):
    u = state_ref[...]
    row = lax.broadcasted_iota(jnp.int32, (ROWS, COLS), 0)
    lane = lax.broadcasted_iota(jnp.int32, (ROWS, COLS), 1)
    beside = jnp.where(row > 0, pltpu.roll(u, 1, 0), 0.0) + jnp.where(row < ROWS - 1, pltpu.roll(u, ROWS - 1, 0), 0.0)
    beside = beside + jnp.where(lane > 0, pltpu.roll(u, 1, 1), 0.0)
    beside = beside + jnp.where(lane < COLS - 1, pltpu.roll(u, COLS - 1, 1), 0.0)
    shaped_ref[...] = (kappa_ref[...] + 4.0) * u - beside


def pack_kernel(own_ref, other_ref, own_extra_ref, other_extra_ref, *outs):
    y, _ = group_place()
    for k in range(GROUPS):
        block = ahead(y, k)
        for slot, (ref, extra) in enumerate(((own_ref, own_extra_ref), (other_ref, other_extra_ref))):
            for r in range(0, ROWS, 8):
                main, side = window(ref, block, slice(r, r + 8))
                outs[k][slot, r : r + 8, :BLOCK] = main
                outs[k][slot, r : r + 8, BLOCK:] = side
            outs[k][slot, ROWS : ROWS + OBS_ROWS, :BLOCK] = extra[:, :BLOCK]
            outs[k][slot, ROWS : ROWS + OBS_ROWS, BLOCK:] = extra[:, pl.ds(pl.multiple_of(BLOCK + block * SIDE, SIDE), SIDE)]


def scatter_kernel(cell_ref, k0, k1, k2, k3, source_ref, near_ref, far_ref, acc):
    y, z = group_place()
    core = lax.rem(lax.axis_index("tile"), 2)
    pieces = (k0, k1, k2, k3)
    acc[...] = jnp.zeros_like(acc)
    rows = lax.broadcasted_iota(jnp.int32, (ROWS, BLOCK), 0)
    lanes = lax.broadcasted_iota(jnp.int32, (WIDE, BLOCK), 0)
    half = SIDE // 2
    for i in range(OBS_ROWS):
        cell = cell_ref[:, i * BLOCK : (i + 1) * BLOCK]
        row = lax.shift_right_logical(cell, 11)
        col = jnp.bitwise_and(cell, COLS - 1) - y * BLOCK
        place = jnp.where(
            (col >= 0) & (col < BLOCK + half), col, jnp.where((col >= -half) & (col < 0), col + WIDE, -1)
        )
        hit_row = rows == row
        hit_col = jnp.where(lanes == place, 1.0, 0.0).astype(jnp.bfloat16)
        highs, lows = [], []
        for k in range(GROUPS):
            for slot in range(2):
                value = pieces[k][slot, ROWS + i : ROWS + i + 1, :BLOCK]
                high = value.astype(jnp.bfloat16).astype(jnp.float32)
                low = value - high
                highs.append(jnp.where(hit_row, high, 0.0).astype(jnp.bfloat16))
                lows.append(jnp.where(hit_row, low, 0.0).astype(jnp.bfloat16))
        values = jnp.concatenate(highs + lows, axis=0)
        acc[...] += lax.dot_general(
            values, hit_col, (((1,), (1,)), ((), ())), preferred_element_type=jnp.float32
        )
    count = VARS * ROWS
    for k in range(GROUPS):
        for slot in range(2):
            at = (k * 2 + slot) * ROWS
            total = acc[at : at + ROWS] + acc[count + at : count + at + ROWS]
            var = 2 * behind(y, k) + lax.rem(z + slot, 2)
            source_ref[var] = total
            near, far = pl.multiple_of(EDGE * (1 - core), EDGE), pl.multiple_of(EDGE * core, EDGE)
            near_ref[var] = source_ref[var, pl.ds(near, EDGE)]
            far_ref[var] = source_ref[var, pl.ds(far, EDGE)]
            near_ref[VARS + var] = pieces[k][slot, pl.ds(near, EDGE)]
            far_ref[VARS + var] = pieces[k][slot, pl.ds(far, EDGE)]
    sub = lax.broadcasted_iota(jnp.int32, (VARS, SIDE), 0)
    for i in range(BLOCK // SIDE):
        held = []
        for e in range(2):
            row = ROWS + e * (BLOCK // SIDE) + i
            rows = jnp.zeros((VARS, SIDE), jnp.float32)
            for k in range(GROUPS):
                for slot in range(2):
                    var = 2 * behind(y, k) + lax.rem(z + slot, 2)
                    rows = jnp.where(sub == var, pieces[k][slot, row : row + 1, BLOCK:], rows)
            held.append(rows)
        near_ref[2 * VARS, :, i * SIDE : (i + 1) * SIDE] = jnp.where(core == 0, held[1], held[0])
        far_ref[2 * VARS, :, i * SIDE : (i + 1) * SIDE] = jnp.where(core == 0, held[0], held[1])
    near_ref[2 * VARS, :, BLOCK:] = jnp.zeros((EDGE, SIDE), jnp.float32)
    far_ref[2 * VARS, :, BLOCK:] = jnp.zeros((EDGE, SIDE), jnp.float32)


def share_kernel(mix_ref, own_ref, other_ref, *outs):
    y, z = group_place()
    for k in range(GROUPS):
        v = 2 * ahead(y, k) + z
        one, two = mix_ref[v, 2 * y + z], mix_ref[v, 2 * y + 1 - z]
        for r in range(0, ROWS, 8):
            outs[k][r : r + 8] = one * own_ref[r : r + 8] + two * other_ref[r : r + 8]


def shape_rows(u):
    return pltpu.roll(u, 1, 0) + pltpu.roll(u, TALL - 1, 0) + pltpu.roll(u, 1, 1) + pltpu.roll(u, WIDE - 1, 1)


def main_kernel(
    mix_ref, source_ref, near_ref, far_ref, k0, k1, k2, k3, adj, kp, res, dirn, tmp, mask_ref
):
    y, z = group_place()
    tile = lax.axis_index("tile")
    pieces = (k0, k1, k2, k3)
    row = lax.broadcasted_iota(jnp.int32, (TALL, WIDE), 0)
    lane = lax.broadcasted_iota(jnp.int32, (TALL, WIDE), 1)
    row = jnp.where(row < ROWS + EDGE, row, row - TALL) + tile * ROWS
    lane = jnp.where(lane < BLOCK + SIDE // 2, lane, lane - WIDE) + y * BLOCK
    inside = (row >= 0) & (row < ROWS * lax.axis_size("tile")) & (lane >= 0) & (lane < COLS)
    mask_ref[...] = jnp.where(inside, 1.0, 0.0)
    mask = mask_ref[...]
    for k in range(GROUPS):
        for slot in range(2):
            var = 2 * behind(y, k) + lax.rem(z + slot, 2)
            kp[var, :ROWS] = pieces[k][slot, :ROWS] + 4.0
    core = lax.rem(tile, 2)
    near, far = pl.multiple_of(ROWS + EDGE * core, EDGE), pl.multiple_of(ROWS + EDGE * (1 - core), EDGE)
    kp[:, pl.ds(near, EDGE)] = near_ref[VARS : 2 * VARS] + 4.0
    kp[:, pl.ds(far, EDGE)] = far_ref[VARS : 2 * VARS] + 4.0
    for var in range(VARS):
        kp[var] = kp[var] * mask_ref[...]
        for at, size, ref in ((0, ROWS, source_ref), (near, EDGE, near_ref), (far, EDGE, far_ref)):
            rows = pl.ds(at, size)
            part = ref[var] * mask_ref[rows]
            res[var, rows] = part
            part = part * (1.0 / THETA)
            dirn[var, rows] = part
            adj[var, rows] = part

    def shape(src, var):
        u = src[var]
        return kp[var] * u - shape_rows(u) * mask_ref[...]

    def couple(ref):
        for r in range(0, TALL, 8):
            fields = [ref[w, r : r + 8] for w in range(VARS)]
            for v in range(VARS):
                total = mix_ref[v, 0] * fields[0]
                for w in range(1, VARS):
                    total = total + mix_ref[v, w] * fields[w]
                ref[v, r : r + 8] = total

    sigma = THETA / DELTA
    rho = 1.0 / sigma
    for _ in range(ITERS - 1):
        rho_new = 1.0 / (2.0 * sigma - rho)
        c1, c2 = rho_new * rho, 2.0 * rho_new / DELTA
        rho = rho_new

        for var in range(VARS):
            tmp[var] = shape(dirn, var)
        couple(tmp)

        for var in range(VARS):
            r = res[var] - shape(tmp, var)
            res[var] = r
            d = c1 * dirn[var] + c2 * r
            dirn[var] = d
            adj[var] = adj[var] + d


def final_kernel(mix_ref, adj, kp, near_ref, far_ref, o0, o1, o2, o3, tmp):
    y, z = group_place()
    core = lax.rem(lax.axis_index("tile"), 2)

    for var in range(VARS):
        u = adj[var]
        tmp[var] = kp[var, :ROWS, :BLOCK] * u[:ROWS, :BLOCK] - shape_rows(u)[:ROWS, :BLOCK]
    for k, out in enumerate((o0, o1, o2, o3)):
        v = 2 * ahead(y, k) + z
        for c in range(0, BLOCK, 128):
            cols = slice(c, c + 128)
            near = mix_ref[v, 0] * near_ref[2 * VARS, 0:1, cols]
            far = mix_ref[v, 0] * far_ref[2 * VARS, 0:1, cols]
            for w in range(1, VARS):
                near = near + mix_ref[v, w] * near_ref[2 * VARS, w : w + 1, cols]
                far = far + mix_ref[v, w] * far_ref[2 * VARS, w : w + 1, cols]
            out[4, 0:1, cols] = jnp.where(core == 0, far, near)
            out[4, 1:2, cols] = jnp.where(core == 0, near, far)
            out[4, 2:, cols] = jnp.zeros((6, 128), jnp.float32)
            for half in range(ROWS // 8):
                rows = slice(half * 8, half * 8 + 8)
                total = mix_ref[v, 0] * tmp[0, rows, cols]
                for w in range(1, VARS):
                    total = total + mix_ref[v, w] * tmp[w, rows, cols]
                out[half, :, cols] = adj[v, rows, cols]
                out[2 + half, :, cols] = total


def join_kernel(p0, p1, p2, p3, m0, m1, m2, m3, state_ref, adjoint_ref, grad_ref):
    y, _ = group_place()
    row = lax.broadcasted_iota(jnp.int32, (8, BLOCK), 0)
    for k, part in enumerate((p0, p1, p2, p3)):
        cols = pl.ds(pl.multiple_of(behind(y, k) * BLOCK, BLOCK), BLOCK)
        for half in range(ROWS // 8):
            rows = slice(half * 8, half * 8 + 8)
            mixed = (m0[rows, cols] + m1[rows, cols]) + (m2[rows, cols] + m3[rows, cols])
            mixed = mixed - jnp.where(row == 7 * half, part[4, half : half + 1], 0.0)
            adjoint_ref[rows, cols] = part[half]
            grad_ref[rows, cols] = -(part[2 + half] * state_ref[rows, cols] + part[half] * mixed)


def call(kernel, outs, n_in, smem=0, scratch=(), flops=1000, size=100000):
    shapes = [jax.ShapeDtypeStruct(s, jnp.float32) for s in outs]
    return pl.pallas_call(
        kernel,
        out_shape=shapes,
        in_specs=[SMEM] * smem + [VMEM] * (n_in - smem),
        out_specs=[VMEM] * len(shapes),
        scratch_shapes=list(scratch),
        compiler_params=pltpu.CompilerParams(vmem_limit_bytes=32 * 1024 * 1024),
        cost_estimate=pl.CostEstimate(flops=flops, bytes_accessed=size, transcendentals=0),
    )


def across(x):
    return lax.ppermute(x, "var", [(i, i ^ 1) for i in range(VARS)])


def around(x, k):
    return lax.ppermute(x, "var", [(i, (i // 2 + k) % GROUPS * 2 + i % 2) for i in range(VARS)])


def beside(x, tiles, near):
    pairs = []
    for i in range(0 if near else 1, tiles - 1, 2):
        for v in range(VARS):
            one, two = i * VARS + v, (i + 1) * VARS + (v ^ 1 if i % 8 == 7 else v)
            pairs += [(one, two), (two, one)]
    return lax.ppermute(x, ("tile", "var"), pairs)


def per_device(tiles, range_sq, state_field, coupling, obs_cell, obs_value):
    mixing = jnp.eye(VARS, dtype=jnp.float32) + coupling
    mix = jnp.einsum("uv,uw->vw", mixing, mixing, precision=lax.Precision.HIGHEST) * (1.0 / 64.0)
    kappa, state = range_sq[0], state_field[0]
    other_kappa = across(kappa)
    (shaped,) = call(shape_kernel, [(ROWS, COLS)], 2)(kappa, state)
    (extra,) = call(extra_kernel, [(8, 2 * BLOCK)], 2)(obs_value, state)
    other_extra = across(extra)
    shaped, _ = lax.optimization_barrier((shaped, other_extra))
    other_shaped = across(shaped)
    pieces = call(pack_kernel, [(2, ROWS + OBS_ROWS, WIDE)] * 4, 4)(kappa, other_kappa, extra, other_extra)
    pieces = [pieces[0]] + [around(pieces[k], k) for k in range(1, GROUPS)]
    edges = (2 * VARS + 1, EDGE, WIDE)
    source, near, far = call(
        scatter_kernel,
        [(VARS, ROWS, WIDE), edges, edges],
        5,
        scratch=[pltpu.VMEM((2 * VARS * ROWS, WIDE), jnp.float32)],
    )(obs_cell.reshape(1, OBS), *pieces)
    far = beside(far, tiles, False)
    near = beside(near, tiles, True)
    shaped, other_shaped, _ = lax.optimization_barrier((shaped, other_shaped, source))
    mixed = call(share_kernel, [(ROWS, COLS)] * 4, 3, smem=1)(mix, shaped, other_shaped)
    mixed = [mixed[0]] + [around(mixed[k], k) for k in range(1, GROUPS)]
    field = (VARS, TALL, WIDE)
    adj, kp = call(
        main_kernel,
        [field] * 2,
        8,
        smem=1,
        scratch=[pltpu.VMEM(field, jnp.float32)] * 3 + [pltpu.VMEM((TALL, WIDE), jnp.float32)],
    )(mix, source, near, far, *pieces)
    parts = call(
        final_kernel,
        [(2 * ROWS // 8 + 1, 8, BLOCK)] * 4,
        5,
        smem=1,
        scratch=[pltpu.VMEM((VARS, ROWS, BLOCK), jnp.float32)],
    )(mix, adj, kp, near, far)
    parts = [parts[0]] + [around(parts[k], k) for k in range(1, GROUPS)]
    adjoint, grad = call(join_kernel, [(ROWS, COLS)] * 2, 9)(*parts, *mixed, state)
    return adjoint[None], grad[None]


def solution(mesh):
    return jax.shard_map(
        functools.partial(per_device, mesh.shape["tile"]),
        mesh=mesh,
        in_specs=(P("var", "tile", None), P("var", "tile", None), P(), P("tile"), P("var", "tile")),
        out_specs=(P("var", "tile", None), P("var", "tile", None)),
        check_vma=False,
    )
```

```python
import functools

import jax
import jax.numpy as jnp
from jax import lax
from jax.experimental import pallas as pl
from jax.experimental.pallas import tpu as pltpu
from jax.sharding import PartitionSpec as P

ITERS = 4
THETA = 4.025
DELTA = 3.975
VMEM = pl.BlockSpec(memory_space=pltpu.VMEM)
SMEM = pl.BlockSpec(memory_space=pltpu.SMEM)

ROWS, COLS, VARS, GROUPS = 16, 2048, 8, 4
BLOCK = COLS // GROUPS
SIDE = 128
WIDE = BLOCK + SIDE
EDGE = 8
TALL = ROWS + 2 * EDGE
OBS = 4096
OBS_ROWS = OBS // BLOCK
SLIM = 16
P_OBS = 4 * BLOCK
P_STATE = P_OBS + 2 * BLOCK
P_SIDE = P_STATE + 2 * SIDE
PIECE = P_SIDE + SIDE
E_SOURCE = VARS * BLOCK
E_SIDE = 2 * VARS * BLOCK
E_STATE = E_SIDE + 2 * SIDE
EDGES = E_STATE + BLOCK


def group_place():
    var = lax.axis_index("var")
    return var // 2, lax.rem(var, 2)


def pack_side(packed, side, index):
    lane = lax.broadcasted_iota(jnp.int32, (8, SIDE), 1)
    here = (lane >= SLIM * index) & (lane < SLIM * index + SLIM)
    return jnp.where(here, pltpu.roll(side, lax.rem(SLIM * index + SLIM // 2, SIDE), 1), packed)


def unpack_side(packed, index):
    return pltpu.roll(packed, lax.rem(2 * SIDE - SLIM // 2 - SLIM * index, SIDE), 1)


def lanes_at(start, size):
    return pl.ds(pl.multiple_of(start, SIDE), size)


def ahead(y, k):
    return lax.rem(y + k, GROUPS)


def behind(y, k):
    return lax.rem(y - k + GROUPS, GROUPS)


def window(ref, block, rows):
    main = ref[rows, pl.ds(pl.multiple_of(block * BLOCK, BLOCK), BLOCK)]
    after = jnp.minimum(block + 1, GROUPS - 1) * BLOCK
    before = jnp.maximum(block * BLOCK - SIDE, 0)
    right = ref[rows, pl.ds(pl.multiple_of(after, SIDE), SIDE)]
    left = ref[rows, pl.ds(pl.multiple_of(before, SIDE), SIDE)]
    lane = lax.broadcasted_iota(jnp.int32, (8, SIDE), 1)
    return main, jnp.where(lane < SIDE // 2, right, left)


def extra_kernel(obs_ref, state_ref, extra_ref):
    for i in range(OBS_ROWS):
        extra_ref[i : i + 1, :BLOCK] = obs_ref[:, i * BLOCK : (i + 1) * BLOCK]
    for e, r in enumerate((0, ROWS - 1)):
        for block in range(GROUPS):
            for i in range(BLOCK // SIDE):
                to, at = e * (BLOCK // SIDE) + i, BLOCK + block * SIDE
                col = block * BLOCK + i * SIDE
                extra_ref[to : to + 1, at : at + SIDE] = state_ref[r : r + 1, col : col + SIDE]


def shape_kernel(kappa_ref, state_ref, shaped_ref):
    u = state_ref[...]
    row = lax.broadcasted_iota(jnp.int32, (ROWS, COLS), 0)
    lane = lax.broadcasted_iota(jnp.int32, (ROWS, COLS), 1)
    beside = jnp.where(row > 0, pltpu.roll(u, 1, 0), 0.0) + jnp.where(row < ROWS - 1, pltpu.roll(u, ROWS - 1, 0), 0.0)
    beside = beside + jnp.where(lane > 0, pltpu.roll(u, 1, 1), 0.0)
    beside = beside + jnp.where(lane < COLS - 1, pltpu.roll(u, COLS - 1, 1), 0.0)
    shaped_ref[...] = (kappa_ref[...] + 4.0) * u - beside


def pack_kernel(own_ref, other_ref, own_extra_ref, other_extra_ref, *outs):
    y, _ = group_place()
    for k in range(GROUPS):
        block = ahead(y, k)
        packed = jnp.zeros((8, SIDE), jnp.float32)
        for slot, (ref, extra) in enumerate(((own_ref, own_extra_ref), (other_ref, other_extra_ref))):
            for half in range(ROWS // 8):
                main, side = window(ref, block, slice(half * 8, half * 8 + 8))
                index = slot * 2 + half
                outs[k][:, index * BLOCK : (index + 1) * BLOCK] = main
                packed = pack_side(packed, side, index)
            outs[k][:, P_OBS + slot * BLOCK : P_OBS + (slot + 1) * BLOCK] = extra[:, :BLOCK]
            state = extra[:, lanes_at(BLOCK + block * SIDE, SIDE)]
            outs[k][:, P_STATE + slot * SIDE : P_STATE + (slot + 1) * SIDE] = state
        outs[k][:, P_SIDE:] = packed


def scatter_kernel(cell_ref, k0, k1, k2, k3, source_ref, near_ref, far_ref, acc):
    y, z = group_place()
    core = lax.rem(lax.axis_index("tile"), 2)
    pieces = (k0, k1, k2, k3)
    acc[...] = jnp.zeros_like(acc)
    rows = lax.broadcasted_iota(jnp.int32, (ROWS, BLOCK), 0)
    lanes = lax.broadcasted_iota(jnp.int32, (WIDE, BLOCK), 0)
    half = SIDE // 2
    for i in range(OBS_ROWS):
        cell = cell_ref[:, i * BLOCK : (i + 1) * BLOCK]
        row = lax.shift_right_logical(cell, 11)
        col = jnp.bitwise_and(cell, COLS - 1) - y * BLOCK
        place = jnp.where(
            (col >= 0) & (col < BLOCK + half), col, jnp.where((col >= -half) & (col < 0), col + WIDE, -1)
        )
        hit_row = rows == row
        hit_col = jnp.where(lanes == place, 1.0, 0.0).astype(jnp.bfloat16)
        highs, lows = [], []
        for k in range(GROUPS):
            for slot in range(2):
                value = pieces[k][i : i + 1, P_OBS + slot * BLOCK : P_OBS + (slot + 1) * BLOCK]
                high = value.astype(jnp.bfloat16).astype(jnp.float32)
                low = value - high
                highs.append(jnp.where(hit_row, high, 0.0).astype(jnp.bfloat16))
                lows.append(jnp.where(hit_row, low, 0.0).astype(jnp.bfloat16))
        values = jnp.concatenate(highs + lows, axis=0)
        acc[...] += lax.dot_general(
            values, hit_col, (((1,), (1,)), ((), ())), preferred_element_type=jnp.float32
        )
    count = VARS * ROWS
    for k in range(GROUPS):
        for slot in range(2):
            at = (k * 2 + slot) * ROWS
            total = acc[at : at + ROWS] + acc[count + at : count + at + ROWS]
            var = 2 * behind(y, k) + lax.rem(z + slot, 2)
            source_ref[var] = total
    for ref, last in ((near_ref, 1 - core), (far_ref, core)):
        packed_kappa = packed_source = jnp.zeros((8, SIDE), jnp.float32)
        for k in range(GROUPS):
            for slot in range(2):
                var = 2 * behind(y, k) + lax.rem(z + slot, 2)
                kappa = pieces[k][:, lanes_at((slot * 2 + last) * BLOCK, BLOCK)]
                ref[:, lanes_at(var * BLOCK, BLOCK)] = kappa
                side = unpack_side(pieces[k][:, P_SIDE:], slot * 2 + last)
                packed_kappa = pack_side(packed_kappa, side, var)
                total = source_ref[var, pl.ds(pl.multiple_of(EDGE * last, EDGE), EDGE)]
                ref[:, lanes_at(E_SOURCE + var * BLOCK, BLOCK)] = total[:, :BLOCK]
                packed_source = pack_side(packed_source, total[:, BLOCK:], var)
        ref[:, E_SIDE : E_SIDE + SIDE] = packed_kappa
        ref[:, E_SIDE + SIDE : E_STATE] = packed_source
    sub = lax.broadcasted_iota(jnp.int32, (VARS, SIDE), 0)
    for i in range(BLOCK // SIDE):
        held = []
        for e in range(2):
            row = e * (BLOCK // SIDE) + i
            rows = jnp.zeros((VARS, SIDE), jnp.float32)
            for k in range(GROUPS):
                for slot in range(2):
                    var = 2 * behind(y, k) + lax.rem(z + slot, 2)
                    at = P_STATE + slot * SIDE
                    rows = jnp.where(sub == var, pieces[k][row : row + 1, at : at + SIDE], rows)
            held.append(rows)
        here = slice(E_STATE + i * SIDE, E_STATE + (i + 1) * SIDE)
        near_ref[:, here] = jnp.where(core == 0, held[1], held[0])
        far_ref[:, here] = jnp.where(core == 0, held[0], held[1])


def share_kernel(mix_ref, own_ref, other_ref, *outs):
    y, z = group_place()
    for k in range(GROUPS):
        v = 2 * ahead(y, k) + z
        one, two = mix_ref[v, 2 * y + z], mix_ref[v, 2 * y + 1 - z]
        for r in range(0, ROWS, 8):
            outs[k][r : r + 8] = one * own_ref[r : r + 8] + two * other_ref[r : r + 8]


def shape_rows(u):
    return pltpu.roll(u, 1, 0) + pltpu.roll(u, TALL - 1, 0) + pltpu.roll(u, 1, 1) + pltpu.roll(u, WIDE - 1, 1)


def main_kernel(
    mix_ref, source_ref, near_ref, far_ref, k0, k1, k2, k3, o0, o1, o2, o3, adj, kp, res, dirn, tmp, mask_ref
):
    y, z = group_place()
    tile = lax.axis_index("tile")
    pieces = (k0, k1, k2, k3)
    row = lax.broadcasted_iota(jnp.int32, (TALL, WIDE), 0)
    lane = lax.broadcasted_iota(jnp.int32, (TALL, WIDE), 1)
    row = jnp.where(row < ROWS + EDGE, row, row - TALL) + tile * ROWS
    lane = jnp.where(lane < BLOCK + SIDE // 2, lane, lane - WIDE) + y * BLOCK
    inside = (row >= 0) & (row < ROWS * lax.axis_size("tile")) & (lane >= 0) & (lane < COLS)
    mask_ref[...] = jnp.where(inside, 1.0, 0.0)
    for k in range(GROUPS):
        for slot in range(2):
            var = 2 * behind(y, k) + lax.rem(z + slot, 2)
            for half in range(ROWS // 8):
                rows, index = slice(half * 8, half * 8 + 8), slot * 2 + half
                mask = mask_ref[rows]
                kappa = pieces[k][:, index * BLOCK : (index + 1) * BLOCK]
                kp[var, rows, :BLOCK] = (kappa + 4.0) * mask[:, :BLOCK]
                kp[var, rows, BLOCK:] = (unpack_side(pieces[k][:, P_SIDE:], index) + 4.0) * mask[:, BLOCK:]
    core = lax.rem(tile, 2)

    def start(var, rows, cols, part):
        res[var, rows, cols] = part
        part = part * (1.0 / THETA)
        dirn[var, rows, cols] = part
        adj[var, rows, cols] = part

    main, edge = slice(0, BLOCK), slice(BLOCK, WIDE)
    for at, ref in ((ROWS + EDGE * core, near_ref), (ROWS + EDGE * (1 - core), far_ref)):
        rows = pl.ds(pl.multiple_of(at, EDGE), EDGE)
        mask = mask_ref[rows]
        for var in range(VARS):
            kp[var, rows, main] = (ref[:, var * BLOCK : (var + 1) * BLOCK] + 4.0) * mask[:, main]
            kp[var, rows, edge] = (unpack_side(ref[:, E_SIDE : E_SIDE + SIDE], var) + 4.0) * mask[:, edge]
            at = E_SOURCE + var * BLOCK
            start(var, rows, main, ref[:, at : at + BLOCK] * mask[:, main])
            start(var, rows, edge, unpack_side(ref[:, E_SIDE + SIDE : E_STATE], var) * mask[:, edge])
    for var in range(VARS):
        start(var, slice(0, ROWS), slice(0, WIDE), source_ref[var] * mask_ref[:ROWS])

    def shape(src, var):
        u = src[var]
        return kp[var] * u - shape_rows(u) * mask_ref[...]

    def couple(ref):
        for r in range(0, TALL, 8):
            fields = [ref[w, r : r + 8] for w in range(VARS)]
            for v in range(VARS):
                total = mix_ref[v, 0] * fields[0]
                for w in range(1, VARS):
                    total = total + mix_ref[v, w] * fields[w]
                ref[v, r : r + 8] = total

    sigma = THETA / DELTA
    rho = 1.0 / sigma
    for _ in range(ITERS - 1):
        rho_new = 1.0 / (2.0 * sigma - rho)
        c1, c2 = rho_new * rho, 2.0 * rho_new / DELTA
        rho = rho_new

        for var in range(VARS):
            tmp[var] = shape(dirn, var)
        couple(tmp)

        for var in range(VARS):
            r = res[var] - shape(tmp, var)
            res[var] = r
            d = c1 * dirn[var] + c2 * r
            dirn[var] = d
            adj[var] = adj[var] + d

    for var in range(VARS):
        u = adj[var]
        tmp[var, :ROWS, :BLOCK] = kp[var, :ROWS, :BLOCK] * u[:ROWS, :BLOCK] - shape_rows(u)[:ROWS, :BLOCK]
    for k, out in enumerate((o0, o1, o2, o3)):
        v = 2 * ahead(y, k) + z
        for c in range(0, BLOCK, 128):
            cols = slice(c, c + 128)
            here = slice(E_STATE + c, E_STATE + c + 128)
            near = mix_ref[v, 0] * near_ref[0:1, here]
            far = mix_ref[v, 0] * far_ref[0:1, here]
            for w in range(1, VARS):
                near = near + mix_ref[v, w] * near_ref[w : w + 1, here]
                far = far + mix_ref[v, w] * far_ref[w : w + 1, here]
            out[4, 0:1, cols] = jnp.where(core == 0, far, near)
            out[4, 1:2, cols] = jnp.where(core == 0, near, far)
            out[4, 2:, cols] = jnp.zeros((6, 128), jnp.float32)
            for half in range(ROWS // 8):
                rows = slice(half * 8, half * 8 + 8)
                total = mix_ref[v, 0] * tmp[0, rows, cols]
                for w in range(1, VARS):
                    total = total + mix_ref[v, w] * tmp[w, rows, cols]
                out[half, :, cols] = adj[v, rows, cols]
                out[2 + half, :, cols] = total


def join_kernel(p0, p1, p2, p3, m0, m1, m2, m3, state_ref, adjoint_ref, grad_ref):
    y, _ = group_place()
    row = lax.broadcasted_iota(jnp.int32, (8, BLOCK), 0)
    for k, part in enumerate((p0, p1, p2, p3)):
        cols = pl.ds(pl.multiple_of(behind(y, k) * BLOCK, BLOCK), BLOCK)
        for half in range(ROWS // 8):
            rows = slice(half * 8, half * 8 + 8)
            mixed = (m0[rows, cols] + m1[rows, cols]) + (m2[rows, cols] + m3[rows, cols])
            mixed = mixed - jnp.where(row == 7 * half, part[4, half : half + 1], 0.0)
            adjoint_ref[rows, cols] = part[half]
            grad_ref[rows, cols] = -(part[2 + half] * state_ref[rows, cols] + part[half] * mixed)


def call(kernel, outs, n_in, smem=0, scratch=(), flops=1000, size=100000):
    shapes = [jax.ShapeDtypeStruct(s, jnp.float32) for s in outs]
    return pl.pallas_call(
        kernel,
        out_shape=shapes,
        in_specs=[SMEM] * smem + [VMEM] * (n_in - smem),
        out_specs=[VMEM] * len(shapes),
        scratch_shapes=list(scratch),
        compiler_params=pltpu.CompilerParams(vmem_limit_bytes=32 * 1024 * 1024),
        cost_estimate=pl.CostEstimate(flops=flops, bytes_accessed=size, transcendentals=0),
    )


def across(x):
    return lax.ppermute(x, "var", [(i, i ^ 1) for i in range(VARS)])


def around(x, k):
    return lax.ppermute(x, "var", [(i, (i // 2 + k) % GROUPS * 2 + i % 2) for i in range(VARS)])


def beside(x, tiles, near):
    pairs = []
    for i in range(0 if near else 1, tiles - 1, 2):
        for v in range(VARS):
            one, two = i * VARS + v, (i + 1) * VARS + (v ^ 1 if i % 8 == 7 else v)
            pairs += [(one, two), (two, one)]
    return lax.ppermute(x, ("tile", "var"), pairs)


def per_device(tiles, range_sq, state_field, coupling, obs_cell, obs_value):
    mixing = jnp.eye(VARS, dtype=jnp.float32) + coupling
    mix = jnp.einsum("uv,uw->vw", mixing, mixing, precision=lax.Precision.HIGHEST) * (1.0 / 64.0)
    kappa, state = range_sq[0], state_field[0]
    other_kappa = across(kappa)
    (shaped,) = call(shape_kernel, [(ROWS, COLS)], 2)(kappa, state)
    (extra,) = call(extra_kernel, [(8, 2 * BLOCK)], 2)(obs_value, state)
    other_extra = across(extra)
    shaped, _ = lax.optimization_barrier((shaped, other_extra))
    other_shaped = across(shaped)
    pieces = call(pack_kernel, [(8, PIECE)] * 4, 4)(kappa, other_kappa, extra, other_extra)
    pieces = [pieces[0]] + [around(pieces[k], k) for k in range(1, GROUPS)]
    edges = (EDGE, EDGES)
    source, near, far = call(
        scatter_kernel,
        [(VARS, ROWS, WIDE), edges, edges],
        5,
        scratch=[pltpu.VMEM((2 * VARS * ROWS, WIDE), jnp.float32)],
    )(obs_cell.reshape(1, OBS), *pieces)
    far = beside(far, tiles, False)
    near = beside(near, tiles, True)
    shaped, other_shaped, _ = lax.optimization_barrier((shaped, other_shaped, source))
    mixed = call(share_kernel, [(ROWS, COLS)] * 4, 3, smem=1)(mix, shaped, other_shaped)
    mixed = [mixed[0]] + [around(mixed[k], k) for k in range(1, GROUPS)]
    field = (VARS, TALL, WIDE)
    parts = call(
        main_kernel,
        [(2 * ROWS // 8 + 1, 8, BLOCK)] * 4,
        8,
        smem=1,
        scratch=[pltpu.VMEM(field, jnp.float32)] * 5 + [pltpu.VMEM((TALL, WIDE), jnp.float32)],
    )(mix, source, near, far, *pieces)
    parts = [parts[0]] + [around(parts[k], k) for k in range(1, GROUPS)]
    adjoint, grad = call(join_kernel, [(ROWS, COLS)] * 2, 9)(*parts, *mixed, state)
    return adjoint[None], grad[None]


def solution(mesh):
    return jax.shard_map(
        functools.partial(per_device, mesh.shape["tile"]),
        mesh=mesh,
        in_specs=(P("var", "tile", None), P("var", "tile", None), P(), P("tile"), P("var", "tile")),
        out_specs=(P("var", "tile", None), P("var", "tile", None)),
        check_vma=False,
    )
```

```python
import functools

import jax
import jax.numpy as jnp
from jax import lax
from jax.experimental import pallas as pl
from jax.experimental.pallas import tpu as pltpu
from jax.sharding import PartitionSpec as P

ITERS = 4
THETA = 4.025
DELTA = 3.975
VMEM = pl.BlockSpec(memory_space=pltpu.VMEM)
SMEM = pl.BlockSpec(memory_space=pltpu.SMEM)

ROWS, COLS, VARS, GROUPS = 16, 2048, 8, 4
BLOCK = COLS // GROUPS
SIDE = 128
WIDE = BLOCK + SIDE
EDGE = 8
TALL = ROWS + 2 * EDGE
OBS = 4096
OBS_ROWS = OBS // BLOCK
EXTRA = ROWS // 8 * COLS
MIB = 1024 * 1024
SLIM = 16
P_OBS = 2 * BLOCK
P_STATE = P_OBS + BLOCK
P_SIDE = P_STATE + SIDE
PIECE = P_SIDE + SIDE
E_SOURCE = VARS * BLOCK
E_SIDE = 2 * VARS * BLOCK
E_STATE = E_SIDE + 2 * SIDE
EDGES = E_STATE + BLOCK


def group_place():
    var = lax.axis_index("var")
    return var // 2, lax.rem(var, 2)


def pack_side(packed, side, index):
    lane = lax.broadcasted_iota(jnp.int32, (8, SIDE), 1)
    here = (lane >= SLIM * index) & (lane < SLIM * index + SLIM)
    return jnp.where(here, pltpu.roll(side, lax.rem(SLIM * index + SLIM // 2, SIDE), 1), packed)


def unpack_side(packed, index):
    return pltpu.roll(packed, lax.rem(2 * SIDE - SLIM // 2 - SLIM * index, SIDE), 1)


def lanes_at(start, size):
    return pl.ds(pl.multiple_of(start, SIDE), size)


def ahead(y, k):
    return lax.rem(y + k, GROUPS)


def behind(y, k):
    return lax.rem(y - k + GROUPS, GROUPS)


def window(ref, block, row):
    start = row * COLS // 8
    main = ref[:, pl.ds(pl.multiple_of(start + block * BLOCK, BLOCK), BLOCK)]
    after = jnp.minimum(block + 1, GROUPS - 1) * BLOCK
    before = jnp.maximum(block * BLOCK - SIDE, 0)
    right = ref[:, pl.ds(pl.multiple_of(start + after, SIDE), SIDE)]
    left = ref[:, pl.ds(pl.multiple_of(start + before, SIDE), SIDE)]
    lane = lax.broadcasted_iota(jnp.int32, (8, SIDE), 1)
    return main, jnp.where(lane < SIDE // 2, right, left)


def first_kernel(kappa_hbm, obs_hbm, state_hbm, sent_ref, kappa_ref, obs_ref, state_ref, sems):
    edges = [(state_hbm.at[r : r + 1, :], state_ref.at[i : i + 1, :]) for i, r in enumerate((0, ROWS - 1))]
    pairs = [(kappa_hbm, kappa_ref), (obs_hbm, obs_ref)] + edges
    copies = [pltpu.make_async_copy(src, dst, sems.at[i]) for i, (src, dst) in enumerate(pairs)]
    for one in copies:
        one.start()
    for one in copies:
        one.wait()
    for r in range(0, ROWS, 8):
        sent_ref[:, r // 8 * COLS : (r // 8 + 1) * COLS] = kappa_ref[r : r + 8]
    for i in range(OBS_ROWS):
        sent_ref[i : i + 1, EXTRA : EXTRA + BLOCK] = obs_ref[:, i * BLOCK : (i + 1) * BLOCK]
    for e in range(2):
        for block in range(GROUPS):
            for i in range(BLOCK // SIDE):
                to, at = e * (BLOCK // SIDE) + i, EXTRA + BLOCK + block * SIDE
                col = block * BLOCK + i * SIDE
                sent_ref[to : to + 1, at : at + SIDE] = state_ref[e : e + 1, col : col + SIDE]


def shape_kernel(kappa_ref, state_ref, shaped_ref):
    u = state_ref[...]
    row = lax.broadcasted_iota(jnp.int32, (ROWS, COLS), 0)
    lane = lax.broadcasted_iota(jnp.int32, (ROWS, COLS), 1)
    beside = jnp.where(row > 0, pltpu.roll(u, 1, 0), 0.0) + jnp.where(row < ROWS - 1, pltpu.roll(u, ROWS - 1, 0), 0.0)
    beside = beside + jnp.where(lane > 0, pltpu.roll(u, 1, 1), 0.0)
    beside = beside + jnp.where(lane < COLS - 1, pltpu.roll(u, COLS - 1, 1), 0.0)
    shaped_ref[...] = (kappa_ref[...] + 4.0) * u - beside


def hold_kernel(sent_ref, held_ref):
    held_ref[...] = sent_ref[...]


def pack_kernel(ref, *outs):
    y, _ = group_place()
    for k in range(GROUPS):
        block = ahead(y, k)
        packed = jnp.zeros((8, SIDE), jnp.float32)
        for half in range(ROWS // 8):
            main, side = window(ref, block, half * 8)
            outs[k][:, half * BLOCK : (half + 1) * BLOCK] = main
            packed = pack_side(packed, side, half)
        outs[k][:, P_OBS:P_STATE] = ref[:, EXTRA : EXTRA + BLOCK]
        outs[k][:, P_STATE:P_SIDE] = ref[:, lanes_at(EXTRA + BLOCK + block * SIDE, SIDE)]
        outs[k][:, P_SIDE:] = packed


def scatter_kernel(cell_ref, *refs):
    y, z = group_place()
    core = lax.rem(lax.axis_index("tile"), 2)
    pieces, (source_ref, near_ref, far_ref, acc) = (refs[:GROUPS], refs[GROUPS : 2 * GROUPS]), refs[2 * GROUPS :]
    acc[...] = jnp.zeros_like(acc)
    rows = lax.broadcasted_iota(jnp.int32, (ROWS, BLOCK), 0)
    lanes = lax.broadcasted_iota(jnp.int32, (WIDE, BLOCK), 0)
    half = SIDE // 2
    for i in range(OBS_ROWS):
        cell = cell_ref[:, i * BLOCK : (i + 1) * BLOCK]
        row = lax.shift_right_logical(cell, 11)
        col = jnp.bitwise_and(cell, COLS - 1) - y * BLOCK
        place = jnp.where(
            (col >= 0) & (col < BLOCK + half), col, jnp.where((col >= -half) & (col < 0), col + WIDE, -1)
        )
        hit_row = rows == row
        hit_col = jnp.where(lanes == place, 1.0, 0.0).astype(jnp.bfloat16)
        highs, lows = [], []
        for k in range(GROUPS):
            for slot in range(2):
                value = pieces[slot][k][i : i + 1, P_OBS:P_STATE]
                high = value.astype(jnp.bfloat16).astype(jnp.float32)
                low = value - high
                highs.append(jnp.where(hit_row, high, 0.0).astype(jnp.bfloat16))
                lows.append(jnp.where(hit_row, low, 0.0).astype(jnp.bfloat16))
        values = jnp.concatenate(highs + lows, axis=0)
        acc[...] += lax.dot_general(
            values, hit_col, (((1,), (1,)), ((), ())), preferred_element_type=jnp.float32
        )
    count = VARS * ROWS
    for k in range(GROUPS):
        for slot in range(2):
            at = (k * 2 + slot) * ROWS
            total = acc[at : at + ROWS] + acc[count + at : count + at + ROWS]
            var = 2 * behind(y, k) + lax.rem(z + slot, 2)
            source_ref[var] = total
    for ref, last in ((near_ref, 1 - core), (far_ref, core)):
        packed_kappa = packed_source = jnp.zeros((8, SIDE), jnp.float32)
        for k in range(GROUPS):
            for slot in range(2):
                var = 2 * behind(y, k) + lax.rem(z + slot, 2)
                kappa = pieces[slot][k][:, lanes_at(last * BLOCK, BLOCK)]
                ref[:, lanes_at(var * BLOCK, BLOCK)] = kappa
                side = unpack_side(pieces[slot][k][:, P_SIDE:], last)
                packed_kappa = pack_side(packed_kappa, side, var)
                total = source_ref[var, pl.ds(pl.multiple_of(EDGE * last, EDGE), EDGE)]
                ref[:, lanes_at(E_SOURCE + var * BLOCK, BLOCK)] = total[:, :BLOCK]
                packed_source = pack_side(packed_source, total[:, BLOCK:], var)
        ref[:, E_SIDE : E_SIDE + SIDE] = packed_kappa
        ref[:, E_SIDE + SIDE : E_STATE] = packed_source
    sub = lax.broadcasted_iota(jnp.int32, (VARS, SIDE), 0)
    for i in range(BLOCK // SIDE):
        held = []
        for e in range(2):
            row = e * (BLOCK // SIDE) + i
            rows = jnp.zeros((VARS, SIDE), jnp.float32)
            for k in range(GROUPS):
                for slot in range(2):
                    var = 2 * behind(y, k) + lax.rem(z + slot, 2)
                    rows = jnp.where(sub == var, pieces[slot][k][row : row + 1, P_STATE:P_SIDE], rows)
            held.append(rows)
        here = slice(E_STATE + i * SIDE, E_STATE + (i + 1) * SIDE)
        near_ref[:, here] = jnp.where(core == 0, held[1], held[0])
        far_ref[:, here] = jnp.where(core == 0, held[0], held[1])


def share_kernel(mix_ref, own_ref, other_ref, *outs):
    y, z = group_place()
    for k in range(GROUPS):
        v = 2 * ahead(y, k) + z
        one, two = mix_ref[v, 2 * y + z], mix_ref[v, 2 * y + 1 - z]
        for r in range(0, ROWS, 8):
            outs[k][r : r + 8] = one * own_ref[r : r + 8] + two * other_ref[r : r + 8]


def shape_rows(u):
    return pltpu.roll(u, 1, 0) + pltpu.roll(u, TALL - 1, 0) + pltpu.roll(u, 1, 1) + pltpu.roll(u, WIDE - 1, 1)


def main_kernel(mix_ref, source_ref, near_ref, far_ref, *refs):
    pieces, outs = (refs[:GROUPS], refs[GROUPS : 2 * GROUPS]), refs[2 * GROUPS : 3 * GROUPS]
    adj, kp, res, dirn, tmp, mask_ref = refs[3 * GROUPS :]
    y, z = group_place()
    tile = lax.axis_index("tile")
    row = lax.broadcasted_iota(jnp.int32, (TALL, WIDE), 0)
    lane = lax.broadcasted_iota(jnp.int32, (TALL, WIDE), 1)
    row = jnp.where(row < ROWS + EDGE, row, row - TALL) + tile * ROWS
    lane = jnp.where(lane < BLOCK + SIDE // 2, lane, lane - WIDE) + y * BLOCK
    inside = (row >= 0) & (row < ROWS * lax.axis_size("tile")) & (lane >= 0) & (lane < COLS)
    mask_ref[...] = jnp.where(inside, 1.0, 0.0)
    for k in range(GROUPS):
        for slot in range(2):
            var = 2 * behind(y, k) + lax.rem(z + slot, 2)
            for half in range(ROWS // 8):
                rows, piece = slice(half * 8, half * 8 + 8), pieces[slot][k]
                mask = mask_ref[rows]
                kappa = piece[:, half * BLOCK : (half + 1) * BLOCK]
                kp[var, rows, :BLOCK] = (kappa + 4.0) * mask[:, :BLOCK]
                kp[var, rows, BLOCK:] = (unpack_side(piece[:, P_SIDE:], half) + 4.0) * mask[:, BLOCK:]
    core = lax.rem(tile, 2)

    def start(var, rows, cols, part):
        res[var, rows, cols] = part
        part = part * (1.0 / THETA)
        dirn[var, rows, cols] = part
        adj[var, rows, cols] = part

    main, edge = slice(0, BLOCK), slice(BLOCK, WIDE)
    for at, ref in ((ROWS + EDGE * core, near_ref), (ROWS + EDGE * (1 - core), far_ref)):
        rows = pl.ds(pl.multiple_of(at, EDGE), EDGE)
        mask = mask_ref[rows]
        for var in range(VARS):
            kp[var, rows, main] = (ref[:, var * BLOCK : (var + 1) * BLOCK] + 4.0) * mask[:, main]
            kp[var, rows, edge] = (unpack_side(ref[:, E_SIDE : E_SIDE + SIDE], var) + 4.0) * mask[:, edge]
            at = E_SOURCE + var * BLOCK
            start(var, rows, main, ref[:, at : at + BLOCK] * mask[:, main])
            start(var, rows, edge, unpack_side(ref[:, E_SIDE + SIDE : E_STATE], var) * mask[:, edge])
    for var in range(VARS):
        start(var, slice(0, ROWS), slice(0, WIDE), source_ref[var] * mask_ref[:ROWS])

    def shape(src, var):
        u = src[var]
        return kp[var] * u - shape_rows(u) * mask_ref[...]

    def couple(ref):
        for r in range(0, TALL, 8):
            fields = [ref[w, r : r + 8] for w in range(VARS)]
            for v in range(VARS):
                total = mix_ref[v, 0] * fields[0]
                for w in range(1, VARS):
                    total = total + mix_ref[v, w] * fields[w]
                ref[v, r : r + 8] = total

    sigma = THETA / DELTA
    rho = 1.0 / sigma
    for _ in range(ITERS - 1):
        rho_new = 1.0 / (2.0 * sigma - rho)
        c1, c2 = rho_new * rho, 2.0 * rho_new / DELTA
        rho = rho_new

        for var in range(VARS):
            tmp[var] = shape(dirn, var)
        couple(tmp)

        for var in range(VARS):
            r = res[var] - shape(tmp, var)
            res[var] = r
            d = c1 * dirn[var] + c2 * r
            dirn[var] = d
            adj[var] = adj[var] + d

    for var in range(VARS):
        u = adj[var]
        tmp[var, :ROWS, :BLOCK] = kp[var, :ROWS, :BLOCK] * u[:ROWS, :BLOCK] - shape_rows(u)[:ROWS, :BLOCK]
    for k, out in enumerate(outs):
        v = 2 * ahead(y, k) + z
        for c in range(0, BLOCK, 128):
            cols = slice(c, c + 128)
            here = slice(E_STATE + c, E_STATE + c + 128)
            near = mix_ref[v, 0] * near_ref[0:1, here]
            far = mix_ref[v, 0] * far_ref[0:1, here]
            for w in range(1, VARS):
                near = near + mix_ref[v, w] * near_ref[w : w + 1, here]
                far = far + mix_ref[v, w] * far_ref[w : w + 1, here]
            out[4, 0:1, cols] = jnp.where(core == 0, far, near)
            out[4, 1:2, cols] = jnp.where(core == 0, near, far)
            out[4, 2:, cols] = jnp.zeros((6, 128), jnp.float32)
            for half in range(ROWS // 8):
                rows = slice(half * 8, half * 8 + 8)
                total = mix_ref[v, 0] * tmp[0, rows, cols]
                for w in range(1, VARS):
                    total = total + mix_ref[v, w] * tmp[w, rows, cols]
                out[half, :, cols] = adj[v, rows, cols]
                out[2 + half, :, cols] = total


def join_kernel(p0, p1, p2, p3, m0, m1, m2, m3, state_ref, adjoint_ref, grad_ref):
    y, _ = group_place()
    row = lax.broadcasted_iota(jnp.int32, (8, BLOCK), 0)
    for k, part in enumerate((p0, p1, p2, p3)):
        cols = pl.ds(pl.multiple_of(behind(y, k) * BLOCK, BLOCK), BLOCK)
        for half in range(ROWS // 8):
            rows = slice(half * 8, half * 8 + 8)
            mixed = (m0[rows, cols] + m1[rows, cols]) + (m2[rows, cols] + m3[rows, cols])
            mixed = mixed - jnp.where(row == 7 * half, part[4, half : half + 1], 0.0)
            adjoint_ref[rows, cols] = part[half]
            grad_ref[rows, cols] = -(part[2 + half] * state_ref[rows, cols] + part[half] * mixed)


def call(kernel, outs, n_in, smem=0, scratch=(), flops=1000, size=100000, hbm=0, limit=32):
    shapes = [jax.ShapeDtypeStruct(s, jnp.float32) for s in outs]
    return pl.pallas_call(
        kernel,
        out_shape=shapes,
        in_specs=[SMEM] * smem + [pl.BlockSpec(memory_space=pl.ANY)] * hbm + [VMEM] * (n_in - smem - hbm),
        out_specs=[VMEM] * len(shapes),
        scratch_shapes=list(scratch),
        compiler_params=pltpu.CompilerParams(vmem_limit_bytes=limit * MIB),
        cost_estimate=pl.CostEstimate(flops=flops, bytes_accessed=size, transcendentals=0),
    )


def across(x):
    return lax.ppermute(x, "var", [(i, i ^ 1) for i in range(VARS)])


def around(x, k):
    return lax.ppermute(x, "var", [(i, (i // 2 + k) % GROUPS * 2 + i % 2) for i in range(VARS)])


def beside(x, tiles, near):
    pairs = []
    for i in range(0 if near else 1, tiles - 1, 2):
        for v in range(VARS):
            one, two = i * VARS + v, (i + 1) * VARS + (v ^ 1 if i % 8 == 7 else v)
            pairs += [(one, two), (two, one)]
    return lax.ppermute(x, ("tile", "var"), pairs)


def per_device(tiles, range_sq, state_field, coupling, obs_cell, obs_value):
    mixing = jnp.eye(VARS, dtype=jnp.float32) + coupling
    mix = jnp.einsum("uv,uw->vw", mixing, mixing, precision=lax.Precision.HIGHEST) * (1.0 / 64.0)
    kappa, state = range_sq[0], state_field[0]
    (sent,) = call(
        first_kernel,
        [(8, EXTRA + 2 * BLOCK)],
        3,
        hbm=3,
        limit=56,
        scratch=[pltpu.VMEM((ROWS, COLS), jnp.float32), pltpu.VMEM((1, OBS), jnp.float32)]
        + [pltpu.VMEM((2, COLS), jnp.float32), pltpu.SemaphoreType.DMA((4,))],
    )(kappa, obs_value, state)
    got = across(sent)
    (sent,) = call(hold_kernel, [(8, EXTRA + 2 * BLOCK)], 1)(sent)
    own = call(pack_kernel, [(8, PIECE)] * 4, 1)(sent)
    own = [own[0]] + [around(own[k], k) for k in range(1, GROUPS)]
    (shaped,) = call(shape_kernel, [(ROWS, COLS)], 2)(kappa, state)
    shaped, own[1] = lax.optimization_barrier((shaped, own[1]))
    other_shaped = across(shaped)
    other = call(pack_kernel, [(8, PIECE)] * 4, 1)(got)
    other = [other[0]] + [around(other[k], k) for k in range(1, GROUPS)]
    pieces = (*own, *other)
    edges = (EDGE, EDGES)
    source, near, far = call(
        scatter_kernel,
        [(VARS, ROWS, WIDE), edges, edges],
        9,
        scratch=[pltpu.VMEM((2 * VARS * ROWS, WIDE), jnp.float32)],
    )(obs_cell.reshape(1, OBS), *pieces)
    far = beside(far, tiles, False)
    shaped, other_shaped, _ = lax.optimization_barrier((shaped, other_shaped, source))
    mixed = call(share_kernel, [(ROWS, COLS)] * 4, 3, smem=1)(mix, shaped, other_shaped)
    near, first = lax.optimization_barrier((near, mixed[0]))
    near = beside(near, tiles, True)
    mixed = [first] + [around(mixed[k], k) for k in range(1, GROUPS)]
    field = (VARS, TALL, WIDE)
    parts = call(
        main_kernel,
        [(2 * ROWS // 8 + 1, 8, BLOCK)] * 4,
        12,
        smem=1,
        scratch=[pltpu.VMEM(field, jnp.float32)] * 5 + [pltpu.VMEM((TALL, WIDE), jnp.float32)],
    )(mix, source, near, far, *pieces)
    parts = [parts[0]] + [around(parts[k], k) for k in range(1, GROUPS)]
    adjoint, grad = call(join_kernel, [(ROWS, COLS)] * 2, 9)(*parts, *mixed, state)
    return adjoint[None], grad[None]


def solution(mesh):
    return jax.shard_map(
        functools.partial(per_device, mesh.shape["tile"]),
        mesh=mesh,
        in_specs=(P("var", "tile", None), P("var", "tile", None), P(), P("tile"), P("var", "tile")),
        out_specs=(P("var", "tile", None), P("var", "tile", None)),
        check_vma=False,
    )
```

```python
import functools

import jax
import jax.numpy as jnp
from jax import lax
from jax.experimental import pallas as pl
from jax.experimental.pallas import tpu as pltpu
from jax.sharding import PartitionSpec as P

ITERS = 4
THETA = 4.025
DELTA = 3.975
VMEM = pl.BlockSpec(memory_space=pltpu.VMEM)
SMEM = pl.BlockSpec(memory_space=pltpu.SMEM)

ROWS, COLS, VARS, GROUPS = 16, 2048, 8, 4
BLOCK = COLS // GROUPS
SIDE = 128
WIDE = BLOCK + SIDE
EDGE = 8
TALL = ROWS + 2 * EDGE
OBS = 4096
OBS_ROWS = OBS // BLOCK
EXTRA = ROWS // 8 * COLS
MIB = 1024 * 1024
SLIM = 16
P_OBS = 2 * BLOCK
P_STATE = P_OBS + BLOCK
P_SIDE = P_STATE + SIDE
PIECE = P_SIDE + SIDE
E_SOURCE = VARS * BLOCK
E_SIDE = 2 * VARS * BLOCK
E_STATE = E_SIDE + 2 * SIDE
EDGES = E_STATE + BLOCK


def group_place():
    var = lax.axis_index("var")
    return var // 2, lax.rem(var, 2)


def pack_side(packed, side, index):
    lane = lax.broadcasted_iota(jnp.int32, (8, SIDE), 1)
    here = (lane >= SLIM * index) & (lane < SLIM * index + SLIM)
    return jnp.where(here, pltpu.roll(side, lax.rem(SLIM * index + SLIM // 2, SIDE), 1), packed)


def unpack_side(packed, index):
    return pltpu.roll(packed, lax.rem(2 * SIDE - SLIM // 2 - SLIM * index, SIDE), 1)


def lanes_at(start, size):
    return pl.ds(pl.multiple_of(start, SIDE), size)


def ahead(y, k):
    return lax.rem(y + k, GROUPS)


def behind(y, k):
    return lax.rem(y - k + GROUPS, GROUPS)


def window(ref, block, row):
    start = row * COLS // 8
    main = ref[:, pl.ds(pl.multiple_of(start + block * BLOCK, BLOCK), BLOCK)]
    after = jnp.minimum(block + 1, GROUPS - 1) * BLOCK
    before = jnp.maximum(block * BLOCK - SIDE, 0)
    right = ref[:, pl.ds(pl.multiple_of(start + after, SIDE), SIDE)]
    left = ref[:, pl.ds(pl.multiple_of(start + before, SIDE), SIDE)]
    lane = lax.broadcasted_iota(jnp.int32, (8, SIDE), 1)
    return main, jnp.where(lane < SIDE // 2, right, left)


def first_kernel(kappa_hbm, obs_hbm, state_hbm, sent_ref, kappa_ref, obs_ref, state_ref, sems):
    edges = [(state_hbm.at[r : r + 1, :], state_ref.at[i : i + 1, :]) for i, r in enumerate((0, ROWS - 1))]
    pairs = [(kappa_hbm, kappa_ref), (obs_hbm, obs_ref)] + edges
    copies = [pltpu.make_async_copy(src, dst, sems.at[i]) for i, (src, dst) in enumerate(pairs)]
    for one in copies:
        one.start()
    for one in copies:
        one.wait()
    for r in range(0, ROWS, 8):
        sent_ref[:, r // 8 * COLS : (r // 8 + 1) * COLS] = kappa_ref[r : r + 8]
    for i in range(OBS_ROWS):
        sent_ref[i : i + 1, EXTRA : EXTRA + BLOCK] = obs_ref[:, i * BLOCK : (i + 1) * BLOCK]
    for e in range(2):
        for block in range(GROUPS):
            for i in range(BLOCK // SIDE):
                to, at = e * (BLOCK // SIDE) + i, EXTRA + BLOCK + block * SIDE
                col = block * BLOCK + i * SIDE
                sent_ref[to : to + 1, at : at + SIDE] = state_ref[e : e + 1, col : col + SIDE]


def shape_kernel(kappa_ref, state_ref, shaped_ref):
    u = state_ref[...]
    row = lax.broadcasted_iota(jnp.int32, (ROWS, COLS), 0)
    lane = lax.broadcasted_iota(jnp.int32, (ROWS, COLS), 1)
    beside = jnp.where(row > 0, pltpu.roll(u, 1, 0), 0.0) + jnp.where(row < ROWS - 1, pltpu.roll(u, ROWS - 1, 0), 0.0)
    beside = beside + jnp.where(lane > 0, pltpu.roll(u, 1, 1), 0.0)
    beside = beside + jnp.where(lane < COLS - 1, pltpu.roll(u, COLS - 1, 1), 0.0)
    shaped_ref[...] = (kappa_ref[...] + 4.0) * u - beside


def hold_kernel(sent_ref, held_ref):
    held_ref[...] = sent_ref[...]


def pack_kernel(ref, *outs):
    y, _ = group_place()
    for k in range(GROUPS):
        block = ahead(y, k)
        packed = jnp.zeros((8, SIDE), jnp.float32)
        for half in range(ROWS // 8):
            main, side = window(ref, block, half * 8)
            outs[k][:, half * BLOCK : (half + 1) * BLOCK] = main
            packed = pack_side(packed, side, half)
        outs[k][:, P_OBS:P_STATE] = ref[:, EXTRA : EXTRA + BLOCK]
        outs[k][:, P_STATE:P_SIDE] = ref[:, lanes_at(EXTRA + BLOCK + block * SIDE, SIDE)]
        outs[k][:, P_SIDE:] = packed


def scatter_kernel(cell_ref, *refs):
    y, z = group_place()
    core = lax.rem(lax.axis_index("tile"), 2)
    pieces, (source_ref, near_ref, far_ref, acc) = (refs[:GROUPS], refs[GROUPS : 2 * GROUPS]), refs[2 * GROUPS :]
    acc[...] = jnp.zeros_like(acc)
    rows = lax.broadcasted_iota(jnp.int32, (ROWS, BLOCK), 0)
    lanes = lax.broadcasted_iota(jnp.int32, (WIDE, BLOCK), 0)
    half = SIDE // 2
    for i in range(OBS_ROWS):
        cell = cell_ref[:, i * BLOCK : (i + 1) * BLOCK]
        row = lax.shift_right_logical(cell, 11)
        col = jnp.bitwise_and(cell, COLS - 1) - y * BLOCK
        place = jnp.where(
            (col >= 0) & (col < BLOCK + half), col, jnp.where((col >= -half) & (col < 0), col + WIDE, -1)
        )
        hit_row = rows == row
        hit_col = jnp.where(lanes == place, 1.0, 0.0).astype(jnp.bfloat16)
        highs, lows = [], []
        for k in range(GROUPS):
            for slot in range(2):
                value = pieces[slot][k][i : i + 1, P_OBS:P_STATE]
                high = value.astype(jnp.bfloat16).astype(jnp.float32)
                low = value - high
                highs.append(jnp.where(hit_row, high, 0.0).astype(jnp.bfloat16))
                lows.append(jnp.where(hit_row, low, 0.0).astype(jnp.bfloat16))
        values = jnp.concatenate(highs + lows, axis=0)
        acc[...] += lax.dot_general(
            values, hit_col, (((1,), (1,)), ((), ())), preferred_element_type=jnp.float32
        )
    count = VARS * ROWS
    for k in range(GROUPS):
        for slot in range(2):
            at = (k * 2 + slot) * ROWS
            total = acc[at : at + ROWS] + acc[count + at : count + at + ROWS]
            var = 2 * behind(y, k) + lax.rem(z + slot, 2)
            source_ref[var] = total
    for ref, last in ((near_ref, 1 - core), (far_ref, core)):
        packed_kappa = packed_source = jnp.zeros((8, SIDE), jnp.float32)
        for k in range(GROUPS):
            for slot in range(2):
                var = 2 * behind(y, k) + lax.rem(z + slot, 2)
                kappa = pieces[slot][k][:, lanes_at(last * BLOCK, BLOCK)]
                ref[:, lanes_at(var * BLOCK, BLOCK)] = kappa
                side = unpack_side(pieces[slot][k][:, P_SIDE:], last)
                packed_kappa = pack_side(packed_kappa, side, var)
                total = source_ref[var, pl.ds(pl.multiple_of(EDGE * last, EDGE), EDGE)]
                ref[:, lanes_at(E_SOURCE + var * BLOCK, BLOCK)] = total[:, :BLOCK]
                packed_source = pack_side(packed_source, total[:, BLOCK:], var)
        ref[:, E_SIDE : E_SIDE + SIDE] = packed_kappa
        ref[:, E_SIDE + SIDE : E_STATE] = packed_source
    sub = lax.broadcasted_iota(jnp.int32, (VARS, SIDE), 0)
    for i in range(BLOCK // SIDE):
        held = []
        for e in range(2):
            row = e * (BLOCK // SIDE) + i
            rows = jnp.zeros((VARS, SIDE), jnp.float32)
            for k in range(GROUPS):
                for slot in range(2):
                    var = 2 * behind(y, k) + lax.rem(z + slot, 2)
                    rows = jnp.where(sub == var, pieces[slot][k][row : row + 1, P_STATE:P_SIDE], rows)
            held.append(rows)
        here = slice(E_STATE + i * SIDE, E_STATE + (i + 1) * SIDE)
        near_ref[:, here] = jnp.where(core == 0, held[1], held[0])
        far_ref[:, here] = jnp.where(core == 0, held[0], held[1])


def share_kernel(mix_ref, own_ref, other_ref, *outs):
    y, z = group_place()
    for k in range(GROUPS):
        v = 2 * ahead(y, k) + z
        one, two = mix_ref[v, 2 * y + z], mix_ref[v, 2 * y + 1 - z]
        for r in range(0, ROWS, 8):
            outs[k][r : r + 8] = one * own_ref[r : r + 8] + two * other_ref[r : r + 8]


def shape_rows(u):
    return pltpu.roll(u, 1, 0) + pltpu.roll(u, TALL - 1, 0) + pltpu.roll(u, 1, 1) + pltpu.roll(u, WIDE - 1, 1)


def far_kernel(far_ref, out_ref):
    out_ref[...] = far_ref[...]


def main_kernel(mix_ref, source_ref, near_ref, far_ref, *refs):
    pieces, outs = (refs[:GROUPS], refs[GROUPS : 2 * GROUPS]), refs[2 * GROUPS : 3 * GROUPS]
    adj, kp, res, dirn, tmp, mask_ref = refs[3 * GROUPS :]
    y, z = group_place()
    tile = lax.axis_index("tile")
    row = lax.broadcasted_iota(jnp.int32, (TALL, WIDE), 0)
    lane = lax.broadcasted_iota(jnp.int32, (TALL, WIDE), 1)
    row = jnp.where(row < ROWS + EDGE, row, row - TALL) + tile * ROWS
    lane = jnp.where(lane < BLOCK + SIDE // 2, lane, lane - WIDE) + y * BLOCK
    inside = (row >= 0) & (row < ROWS * lax.axis_size("tile")) & (lane >= 0) & (lane < COLS)
    mask_ref[...] = jnp.where(inside, 1.0, 0.0)
    for k in range(GROUPS):
        for slot in range(2):
            var = 2 * behind(y, k) + lax.rem(z + slot, 2)
            for half in range(ROWS // 8):
                rows, piece = slice(half * 8, half * 8 + 8), pieces[slot][k]
                mask = mask_ref[rows]
                kappa = piece[:, half * BLOCK : (half + 1) * BLOCK]
                kp[var, rows, :BLOCK] = (kappa + 4.0) * mask[:, :BLOCK]
                kp[var, rows, BLOCK:] = (unpack_side(piece[:, P_SIDE:], half) + 4.0) * mask[:, BLOCK:]
    core = lax.rem(tile, 2)

    def start(var, rows, cols, part):
        res[var, rows, cols] = part
        part = part * (1.0 / THETA)
        dirn[var, rows, cols] = part
        adj[var, rows, cols] = part

    main, edge = slice(0, BLOCK), slice(BLOCK, WIDE)
    for at, ref in ((ROWS + EDGE * core, near_ref), (ROWS + EDGE * (1 - core), far_ref)):
        rows = pl.ds(pl.multiple_of(at, EDGE), EDGE)
        mask = mask_ref[rows]
        for var in range(VARS):
            kp[var, rows, main] = (ref[:, var * BLOCK : (var + 1) * BLOCK] + 4.0) * mask[:, main]
            kp[var, rows, edge] = (unpack_side(ref[:, E_SIDE : E_SIDE + SIDE], var) + 4.0) * mask[:, edge]
            at = E_SOURCE + var * BLOCK
            start(var, rows, main, ref[:, at : at + BLOCK] * mask[:, main])
            start(var, rows, edge, unpack_side(ref[:, E_SIDE + SIDE : E_STATE], var) * mask[:, edge])
    for var in range(VARS):
        start(var, slice(0, ROWS), slice(0, WIDE), source_ref[var] * mask_ref[:ROWS])

    def shape(src, var):
        u = src[var]
        return kp[var] * u - shape_rows(u) * mask_ref[...]

    def couple(ref):
        for r in range(0, TALL, 8):
            fields = [ref[w, r : r + 8] for w in range(VARS)]
            for v in range(VARS):
                total = mix_ref[v, 0] * fields[0]
                for w in range(1, VARS):
                    total = total + mix_ref[v, w] * fields[w]
                ref[v, r : r + 8] = total

    sigma = THETA / DELTA
    rho = 1.0 / sigma
    for _ in range(ITERS - 1):
        rho_new = 1.0 / (2.0 * sigma - rho)
        c1, c2 = rho_new * rho, 2.0 * rho_new / DELTA
        rho = rho_new

        for var in range(VARS):
            tmp[var] = shape(dirn, var)
        couple(tmp)

        for var in range(VARS):
            r = res[var] - shape(tmp, var)
            res[var] = r
            d = c1 * dirn[var] + c2 * r
            dirn[var] = d
            adj[var] = adj[var] + d

    for var in range(VARS):
        u = adj[var]
        tmp[var, :ROWS, :BLOCK] = kp[var, :ROWS, :BLOCK] * u[:ROWS, :BLOCK] - shape_rows(u)[:ROWS, :BLOCK]
    for k, out in enumerate(outs):
        v = 2 * ahead(y, k) + z
        for c in range(0, BLOCK, 128):
            cols = slice(c, c + 128)
            here = slice(E_STATE + c, E_STATE + c + 128)
            near = mix_ref[v, 0] * near_ref[0:1, here]
            far = mix_ref[v, 0] * far_ref[0:1, here]
            for w in range(1, VARS):
                near = near + mix_ref[v, w] * near_ref[w : w + 1, here]
                far = far + mix_ref[v, w] * far_ref[w : w + 1, here]
            out[4, 0:1, cols] = jnp.where(core == 0, far, near)
            out[4, 1:2, cols] = jnp.where(core == 0, near, far)
            out[4, 2:, cols] = jnp.zeros((6, 128), jnp.float32)
            for half in range(ROWS // 8):
                rows = slice(half * 8, half * 8 + 8)
                total = mix_ref[v, 0] * tmp[0, rows, cols]
                for w in range(1, VARS):
                    total = total + mix_ref[v, w] * tmp[w, rows, cols]
                out[half, :, cols] = adj[v, rows, cols]
                out[2 + half, :, cols] = total


def join_kernel(p0, p1, p2, p3, m0, m1, m2, m3, state_ref, adjoint_ref, grad_ref):
    y, _ = group_place()
    row = lax.broadcasted_iota(jnp.int32, (8, BLOCK), 0)
    for k, part in enumerate((p0, p1, p2, p3)):
        cols = pl.ds(pl.multiple_of(behind(y, k) * BLOCK, BLOCK), BLOCK)
        for half in range(ROWS // 8):
            rows = slice(half * 8, half * 8 + 8)
            mixed = (m0[rows, cols] + m1[rows, cols]) + (m2[rows, cols] + m3[rows, cols])
            mixed = mixed - jnp.where(row == 7 * half, part[4, half : half + 1], 0.0)
            adjoint_ref[rows, cols] = part[half]
            grad_ref[rows, cols] = -(part[2 + half] * state_ref[rows, cols] + part[half] * mixed)


def call(kernel, outs, n_in, smem=0, scratch=(), flops=1000, size=100000, hbm=0, limit=32):
    shapes = [jax.ShapeDtypeStruct(s, jnp.float32) for s in outs]
    return pl.pallas_call(
        kernel,
        out_shape=shapes,
        in_specs=[SMEM] * smem + [pl.BlockSpec(memory_space=pl.ANY)] * hbm + [VMEM] * (n_in - smem - hbm),
        out_specs=[VMEM] * len(shapes),
        scratch_shapes=list(scratch),
        compiler_params=pltpu.CompilerParams(vmem_limit_bytes=limit * MIB),
        cost_estimate=pl.CostEstimate(flops=flops, bytes_accessed=size, transcendentals=0),
    )


def across(x):
    return lax.ppermute(x, "var", [(i, i ^ 1) for i in range(VARS)])


def around(x, k):
    return lax.ppermute(x, "var", [(i, (i // 2 + k) % GROUPS * 2 + i % 2) for i in range(VARS)])


def beside(x, tiles, near):
    pairs = []
    for i in range(0 if near else 1, tiles - 1, 2):
        for v in range(VARS):
            one, two = i * VARS + v, (i + 1) * VARS + (v ^ 1 if i % 8 == 7 else v)
            pairs += [(one, two), (two, one)]
    return lax.ppermute(x, ("tile", "var"), pairs)


def per_device(tiles, range_sq, state_field, coupling, obs_cell, obs_value):
    mixing = jnp.eye(VARS, dtype=jnp.float32) + coupling
    mix = jnp.einsum("uv,uw->vw", mixing, mixing, precision=lax.Precision.HIGHEST) * (1.0 / 64.0)
    kappa, state = range_sq[0], state_field[0]
    (sent,) = call(
        first_kernel,
        [(8, EXTRA + 2 * BLOCK)],
        3,
        hbm=3,
        limit=56,
        scratch=[pltpu.VMEM((ROWS, COLS), jnp.float32), pltpu.VMEM((1, OBS), jnp.float32)]
        + [pltpu.VMEM((2, COLS), jnp.float32), pltpu.SemaphoreType.DMA((4,))],
    )(kappa, obs_value, state)
    got = across(sent)
    (sent,) = call(hold_kernel, [(8, EXTRA + 2 * BLOCK)], 1)(sent)
    own = call(pack_kernel, [(8, PIECE)] * 4, 1)(sent)
    own = [own[0]] + [around(own[k], k) for k in range(1, GROUPS)]
    (shaped,) = call(shape_kernel, [(ROWS, COLS)], 2)(kappa, state)
    shaped, own[1] = lax.optimization_barrier((shaped, own[1]))
    other_shaped = across(shaped)
    other = call(pack_kernel, [(8, PIECE)] * 4, 1)(got)
    other = [other[0]] + [around(other[k], k) for k in range(1, GROUPS)]
    pieces = (*own, *other)
    edges = (EDGE, EDGES)
    source, near, far = call(
        scatter_kernel,
        [(VARS, ROWS, WIDE), edges, edges],
        9,
        scratch=[pltpu.VMEM((2 * VARS * ROWS, WIDE), jnp.float32)],
    )(obs_cell.reshape(1, OBS), *pieces)
    far, other_shaped = lax.optimization_barrier((far, other_shaped))
    far = beside(far, tiles, False)
    shaped, other_shaped, _ = lax.optimization_barrier((shaped, other_shaped, source))
    mixed = call(share_kernel, [(ROWS, COLS)] * 4, 3, smem=1)(mix, shaped, other_shaped)
    near, first = lax.optimization_barrier((near, mixed[0]))
    near = beside(near, tiles, True)
    mixed = [first] + [around(mixed[k], k) for k in range(1, GROUPS)]
    (far,) = call(far_kernel, [edges], 1, flops=1_000_000_000)(far)
    field = (VARS, TALL, WIDE)
    parts = call(
        main_kernel,
        [(2 * ROWS // 8 + 1, 8, BLOCK)] * 4,
        12,
        smem=1,
        scratch=[pltpu.VMEM(field, jnp.float32)] * 5 + [pltpu.VMEM((TALL, WIDE), jnp.float32)],
    )(mix, source, near, far, *pieces)
    parts = [parts[0]] + [around(parts[k], k) for k in range(1, GROUPS)]
    adjoint, grad = call(join_kernel, [(ROWS, COLS)] * 2, 9)(*parts, *mixed, state)
    return adjoint[None], grad[None]


def solution(mesh):
    return jax.shard_map(
        functools.partial(per_device, mesh.shape["tile"]),
        mesh=mesh,
        in_specs=(P("var", "tile", None), P("var", "tile", None), P(), P("tile"), P("var", "tile")),
        out_specs=(P("var", "tile", None), P("var", "tile", None)),
        check_vma=False,
    )
```

```python
import functools

import jax
import jax.numpy as jnp
from jax import lax
from jax.experimental import pallas as pl
from jax.experimental.pallas import tpu as pltpu
from jax.sharding import PartitionSpec as P

ITERS = 4
THETA = 4.025
DELTA = 3.975
VMEM = pl.BlockSpec(memory_space=pltpu.VMEM)
SMEM = pl.BlockSpec(memory_space=pltpu.SMEM)

ROWS, COLS, VARS, GROUPS = 16, 2048, 8, 4
BLOCK = COLS // GROUPS
SIDE = 128
WIDE = BLOCK + SIDE
EDGE = 8
TALL = ROWS + 2 * EDGE
OBS = 4096
OBS_ROWS = OBS // BLOCK
EXTRA = ROWS // 8 * COLS
MIB = 1024 * 1024
SLIM = 16
P_OBS = 2 * BLOCK
P_STATE = P_OBS + BLOCK
P_SIDE = P_STATE + SIDE
PIECE = P_SIDE + SIDE
E_SOURCE = VARS * BLOCK
E_SIDE = 2 * VARS * BLOCK
E_STATE = E_SIDE + 2 * SIDE
EDGES = E_STATE + BLOCK


def group_place():
    var = lax.axis_index("var")
    return var // 2, lax.rem(var, 2)


def pack_side(packed, side, index):
    lane = lax.broadcasted_iota(jnp.int32, (8, SIDE), 1)
    here = (lane >= SLIM * index) & (lane < SLIM * index + SLIM)
    return jnp.where(here, pltpu.roll(side, lax.rem(SLIM * index + SLIM // 2, SIDE), 1), packed)


def unpack_side(packed, index):
    return pltpu.roll(packed, lax.rem(2 * SIDE - SLIM // 2 - SLIM * index, SIDE), 1)


def lanes_at(start, size):
    return pl.ds(pl.multiple_of(start, SIDE), size)


def ahead(y, k):
    return lax.rem(y + k, GROUPS)


def behind(y, k):
    return lax.rem(y - k + GROUPS, GROUPS)


def window(ref, block, row):
    start = row * COLS // 8
    main = ref[:, pl.ds(pl.multiple_of(start + block * BLOCK, BLOCK), BLOCK)]
    after = jnp.minimum(block + 1, GROUPS - 1) * BLOCK
    before = jnp.maximum(block * BLOCK - SIDE, 0)
    right = ref[:, pl.ds(pl.multiple_of(start + after, SIDE), SIDE)]
    left = ref[:, pl.ds(pl.multiple_of(start + before, SIDE), SIDE)]
    lane = lax.broadcasted_iota(jnp.int32, (8, SIDE), 1)
    return main, jnp.where(lane < SIDE // 2, right, left)


def first_kernel(kappa_hbm, obs_hbm, state_hbm, sent_ref, kappa_ref, obs_ref, state_ref, sems):
    edges = [(state_hbm.at[r : r + 1, :], state_ref.at[i : i + 1, :]) for i, r in enumerate((0, ROWS - 1))]
    pairs = [(kappa_hbm, kappa_ref), (obs_hbm, obs_ref)] + edges
    copies = [pltpu.make_async_copy(src, dst, sems.at[i]) for i, (src, dst) in enumerate(pairs)]
    for one in copies:
        one.start()
    for one in copies:
        one.wait()
    for r in range(0, ROWS, 8):
        sent_ref[:, r // 8 * COLS : (r // 8 + 1) * COLS] = kappa_ref[r : r + 8]
    for i in range(OBS_ROWS):
        sent_ref[i : i + 1, EXTRA : EXTRA + BLOCK] = obs_ref[:, i * BLOCK : (i + 1) * BLOCK]
    for e in range(2):
        for block in range(GROUPS):
            for i in range(BLOCK // SIDE):
                to, at = e * (BLOCK // SIDE) + i, EXTRA + BLOCK + block * SIDE
                col = block * BLOCK + i * SIDE
                sent_ref[to : to + 1, at : at + SIDE] = state_ref[e : e + 1, col : col + SIDE]


def shape_kernel(kappa_ref, state_ref, shaped_ref):
    u = state_ref[...]
    row = lax.broadcasted_iota(jnp.int32, (ROWS, COLS), 0)
    lane = lax.broadcasted_iota(jnp.int32, (ROWS, COLS), 1)
    beside = jnp.where(row > 0, pltpu.roll(u, 1, 0), 0.0) + jnp.where(row < ROWS - 1, pltpu.roll(u, ROWS - 1, 0), 0.0)
    beside = beside + jnp.where(lane > 0, pltpu.roll(u, 1, 1), 0.0)
    beside = beside + jnp.where(lane < COLS - 1, pltpu.roll(u, COLS - 1, 1), 0.0)
    shaped_ref[...] = (kappa_ref[...] + 4.0) * u - beside


def hold_kernel(sent_ref, held_ref):
    held_ref[...] = sent_ref[...]


def pack_kernel(ref, *outs):
    y, _ = group_place()
    for k in range(GROUPS):
        block = ahead(y, k)
        packed = jnp.zeros((8, SIDE), jnp.float32)
        for half in range(ROWS // 8):
            main, side = window(ref, block, half * 8)
            outs[k][:, half * BLOCK : (half + 1) * BLOCK] = main
            packed = pack_side(packed, side, half)
        outs[k][:, P_OBS:P_STATE] = ref[:, EXTRA : EXTRA + BLOCK]
        outs[k][:, P_STATE:P_SIDE] = ref[:, lanes_at(EXTRA + BLOCK + block * SIDE, SIDE)]
        outs[k][:, P_SIDE:] = packed


def scatter_kernel(cell_ref, *refs):
    y, z = group_place()
    core = lax.rem(lax.axis_index("tile"), 2)
    pieces, (source_ref, near_ref, far_ref, acc) = (refs[:GROUPS], refs[GROUPS : 2 * GROUPS]), refs[2 * GROUPS :]
    acc[...] = jnp.zeros_like(acc)
    rows = lax.broadcasted_iota(jnp.int32, (ROWS, BLOCK), 0)
    lanes = lax.broadcasted_iota(jnp.int32, (WIDE, BLOCK), 0)
    half = SIDE // 2
    for i in range(OBS_ROWS):
        cell = cell_ref[:, i * BLOCK : (i + 1) * BLOCK]
        row = lax.shift_right_logical(cell, 11)
        col = jnp.bitwise_and(cell, COLS - 1) - y * BLOCK
        place = jnp.where(
            (col >= 0) & (col < BLOCK + half), col, jnp.where((col >= -half) & (col < 0), col + WIDE, -1)
        )
        hit_row = rows == row
        hit_col = jnp.where(lanes == place, 1.0, 0.0).astype(jnp.bfloat16)
        highs, lows = [], []
        for k in range(GROUPS):
            for slot in range(2):
                value = pieces[slot][k][i : i + 1, P_OBS:P_STATE]
                high = value.astype(jnp.bfloat16).astype(jnp.float32)
                low = value - high
                highs.append(jnp.where(hit_row, high, 0.0).astype(jnp.bfloat16))
                lows.append(jnp.where(hit_row, low, 0.0).astype(jnp.bfloat16))
        values = jnp.concatenate(highs + lows, axis=0)
        acc[...] += lax.dot_general(
            values, hit_col, (((1,), (1,)), ((), ())), preferred_element_type=jnp.float32
        )
    count = VARS * ROWS
    for k in range(GROUPS):
        for slot in range(2):
            at = (k * 2 + slot) * ROWS
            total = acc[at : at + ROWS] + acc[count + at : count + at + ROWS]
            var = 2 * behind(y, k) + lax.rem(z + slot, 2)
            source_ref[var] = total
    for ref, last in ((near_ref, 1 - core), (far_ref, core)):
        packed_kappa = packed_source = jnp.zeros((8, SIDE), jnp.float32)
        for k in range(GROUPS):
            for slot in range(2):
                var = 2 * behind(y, k) + lax.rem(z + slot, 2)
                kappa = pieces[slot][k][:, lanes_at(last * BLOCK, BLOCK)]
                ref[:, lanes_at(var * BLOCK, BLOCK)] = kappa
                side = unpack_side(pieces[slot][k][:, P_SIDE:], last)
                packed_kappa = pack_side(packed_kappa, side, var)
                total = source_ref[var, pl.ds(pl.multiple_of(EDGE * last, EDGE), EDGE)]
                ref[:, lanes_at(E_SOURCE + var * BLOCK, BLOCK)] = total[:, :BLOCK]
                packed_source = pack_side(packed_source, total[:, BLOCK:], var)
        ref[:, E_SIDE : E_SIDE + SIDE] = packed_kappa
        ref[:, E_SIDE + SIDE : E_STATE] = packed_source
    sub = lax.broadcasted_iota(jnp.int32, (VARS, SIDE), 0)
    for i in range(BLOCK // SIDE):
        held = []
        for e in range(2):
            row = e * (BLOCK // SIDE) + i
            rows = jnp.zeros((VARS, SIDE), jnp.float32)
            for k in range(GROUPS):
                for slot in range(2):
                    var = 2 * behind(y, k) + lax.rem(z + slot, 2)
                    rows = jnp.where(sub == var, pieces[slot][k][row : row + 1, P_STATE:P_SIDE], rows)
            held.append(rows)
        here = slice(E_STATE + i * SIDE, E_STATE + (i + 1) * SIDE)
        near_ref[:, here] = jnp.where(core == 0, held[1], held[0])
        far_ref[:, here] = jnp.where(core == 0, held[0], held[1])


def share_kernel(mix_ref, own_ref, other_ref, *outs):
    y, z = group_place()
    for k in range(GROUPS):
        v = 2 * ahead(y, k) + z
        one, two = mix_ref[v, 2 * y + z], mix_ref[v, 2 * y + 1 - z]
        for r in range(0, ROWS, 8):
            outs[k][r : r + 8] = one * own_ref[r : r + 8] + two * other_ref[r : r + 8]


def shape_rows(u):
    return pltpu.roll(u, 1, 0) + pltpu.roll(u, TALL - 1, 0) + pltpu.roll(u, 1, 1) + pltpu.roll(u, WIDE - 1, 1)


def far_kernel(far_ref, out_ref):
    out_ref[...] = far_ref[...]


def main_kernel(mix_ref, source_ref, near_ref, far_ref, *refs):
    pieces, outs = (refs[:GROUPS], refs[GROUPS : 2 * GROUPS]), refs[2 * GROUPS : 3 * GROUPS]
    adj, kp, res, dirn, tmp, mask_ref = refs[3 * GROUPS :]
    y, z = group_place()
    tile = lax.axis_index("tile")
    row = lax.broadcasted_iota(jnp.int32, (TALL, WIDE), 0)
    lane = lax.broadcasted_iota(jnp.int32, (TALL, WIDE), 1)
    row = jnp.where(row < ROWS + EDGE, row, row - TALL) + tile * ROWS
    lane = jnp.where(lane < BLOCK + SIDE // 2, lane, lane - WIDE) + y * BLOCK
    inside = (row >= 0) & (row < ROWS * lax.axis_size("tile")) & (lane >= 0) & (lane < COLS)
    mask_ref[...] = jnp.where(inside, 1.0, 0.0)
    for k in range(GROUPS):
        for slot in range(2):
            var = 2 * behind(y, k) + lax.rem(z + slot, 2)
            for half in range(ROWS // 8):
                rows, piece = slice(half * 8, half * 8 + 8), pieces[slot][k]
                mask = mask_ref[rows]
                kappa = piece[:, half * BLOCK : (half + 1) * BLOCK]
                kp[var, rows, :BLOCK] = (kappa + 4.0) * mask[:, :BLOCK]
                kp[var, rows, BLOCK:] = (unpack_side(piece[:, P_SIDE:], half) + 4.0) * mask[:, BLOCK:]
    core = lax.rem(tile, 2)

    def start(var, rows, cols, part):
        res[var, rows, cols] = part
        part = part * (1.0 / THETA)
        dirn[var, rows, cols] = part
        adj[var, rows, cols] = part

    main, edge = slice(0, BLOCK), slice(BLOCK, WIDE)
    for at, ref in ((ROWS + EDGE * core, near_ref), (ROWS + EDGE * (1 - core), far_ref)):
        rows = pl.ds(pl.multiple_of(at, EDGE), EDGE)
        mask = mask_ref[rows]
        for var in range(VARS):
            kp[var, rows, main] = (ref[:, var * BLOCK : (var + 1) * BLOCK] + 4.0) * mask[:, main]
            kp[var, rows, edge] = (unpack_side(ref[:, E_SIDE : E_SIDE + SIDE], var) + 4.0) * mask[:, edge]
            at = E_SOURCE + var * BLOCK
            start(var, rows, main, ref[:, at : at + BLOCK] * mask[:, main])
            start(var, rows, edge, unpack_side(ref[:, E_SIDE + SIDE : E_STATE], var) * mask[:, edge])
    for var in range(VARS):
        start(var, slice(0, ROWS), slice(0, WIDE), source_ref[var] * mask_ref[:ROWS])

    def shape(src, var):
        u = src[var]
        return kp[var] * u - shape_rows(u) * mask_ref[...]

    def couple(ref):
        for r in range(0, TALL, 8):
            fields = [ref[w, r : r + 8] for w in range(VARS)]
            for v in range(VARS):
                total = mix_ref[v, 0] * fields[0]
                for w in range(1, VARS):
                    total = total + mix_ref[v, w] * fields[w]
                ref[v, r : r + 8] = total

    sigma = THETA / DELTA
    rho = 1.0 / sigma
    for _ in range(ITERS - 1):
        rho_new = 1.0 / (2.0 * sigma - rho)
        c1, c2 = rho_new * rho, 2.0 * rho_new / DELTA
        rho = rho_new

        for var in range(VARS):
            tmp[var] = shape(dirn, var)
        couple(tmp)

        for var in range(VARS):
            r = res[var] - shape(tmp, var)
            res[var] = r
            d = c1 * dirn[var] + c2 * r
            dirn[var] = d
            adj[var] = adj[var] + d

    for var in range(VARS):
        u = adj[var]
        tmp[var, :ROWS, :BLOCK] = kp[var, :ROWS, :BLOCK] * u[:ROWS, :BLOCK] - shape_rows(u)[:ROWS, :BLOCK]
    for k, out in enumerate(outs):
        v = 2 * ahead(y, k) + z
        for c in range(0, BLOCK, 128):
            cols = slice(c, c + 128)
            here = slice(E_STATE + c, E_STATE + c + 128)
            near = mix_ref[v, 0] * near_ref[0:1, here]
            far = mix_ref[v, 0] * far_ref[0:1, here]
            for w in range(1, VARS):
                near = near + mix_ref[v, w] * near_ref[w : w + 1, here]
                far = far + mix_ref[v, w] * far_ref[w : w + 1, here]
            i = c // SIDE
            out[i : i + 1, 4 * BLOCK :] = jnp.where(core == 0, far, near)
            out[4 + i : 5 + i, 4 * BLOCK :] = jnp.where(core == 0, near, far)
            for half in range(ROWS // 8):
                rows = slice(half * 8, half * 8 + 8)
                total = mix_ref[v, 0] * tmp[0, rows, cols]
                for w in range(1, VARS):
                    total = total + mix_ref[v, w] * tmp[w, rows, cols]
                out[:, half * BLOCK + c : half * BLOCK + c + 128] = adj[v, rows, cols]
                out[:, (2 + half) * BLOCK + c : (2 + half) * BLOCK + c + 128] = total


def join_kernel(p0, p1, p2, p3, m0, m1, m2, m3, state_ref, adjoint_ref, grad_ref):
    y, _ = group_place()
    row = lax.broadcasted_iota(jnp.int32, (8, SIDE), 0)
    for k, part in enumerate((p0, p1, p2, p3)):
        for half in range(ROWS // 8):
            rows = slice(half * 8, half * 8 + 8)
            for i in range(BLOCK // SIDE):
                cols = lanes_at(behind(y, k) * BLOCK + i * SIDE, SIDE)
                mixed = (m0[rows, cols] + m1[rows, cols]) + (m2[rows, cols] + m3[rows, cols])
                edge = 4 * half + i
                mixed = mixed - jnp.where(row == 7 * half, part[edge : edge + 1, 4 * BLOCK :], 0.0)
                at = half * BLOCK + i * SIDE
                adjoint = part[:, at : at + SIDE]
                at += 2 * BLOCK
                adjoint_ref[rows, cols] = adjoint
                grad_ref[rows, cols] = -(part[:, at : at + SIDE] * state_ref[rows, cols] + adjoint * mixed)


def call(kernel, outs, n_in, smem=0, scratch=(), flops=1000, size=100000, hbm=0, limit=32):
    shapes = [jax.ShapeDtypeStruct(s, jnp.float32) for s in outs]
    return pl.pallas_call(
        kernel,
        out_shape=shapes,
        in_specs=[SMEM] * smem + [pl.BlockSpec(memory_space=pl.ANY)] * hbm + [VMEM] * (n_in - smem - hbm),
        out_specs=[VMEM] * len(shapes),
        scratch_shapes=list(scratch),
        compiler_params=pltpu.CompilerParams(vmem_limit_bytes=limit * MIB),
        cost_estimate=pl.CostEstimate(flops=flops, bytes_accessed=size, transcendentals=0),
    )


def across(x):
    return lax.ppermute(x, "var", [(i, i ^ 1) for i in range(VARS)])


def around(x, k):
    return lax.ppermute(x, "var", [(i, (i // 2 + k) % GROUPS * 2 + i % 2) for i in range(VARS)])


def beside(x, tiles, near):
    pairs = []
    for i in range(0 if near else 1, tiles - 1, 2):
        for v in range(VARS):
            one, two = i * VARS + v, (i + 1) * VARS + (v ^ 1 if i % 8 == 7 else v)
            pairs += [(one, two), (two, one)]
    return lax.ppermute(x, ("tile", "var"), pairs)


def per_device(tiles, range_sq, state_field, coupling, obs_cell, obs_value):
    mixing = jnp.eye(VARS, dtype=jnp.float32) + coupling
    mix = jnp.einsum("uv,uw->vw", mixing, mixing, precision=lax.Precision.HIGHEST) * (1.0 / 64.0)
    kappa, state = range_sq[0], state_field[0]
    (sent,) = call(
        first_kernel,
        [(8, EXTRA + 2 * BLOCK)],
        3,
        hbm=3,
        limit=56,
        scratch=[pltpu.VMEM((ROWS, COLS), jnp.float32), pltpu.VMEM((1, OBS), jnp.float32)]
        + [pltpu.VMEM((2, COLS), jnp.float32), pltpu.SemaphoreType.DMA((4,))],
    )(kappa, obs_value, state)
    got = across(sent)
    (sent,) = call(hold_kernel, [(8, EXTRA + 2 * BLOCK)], 1)(sent)
    own = call(pack_kernel, [(8, PIECE)] * 4, 1)(sent)
    own = [own[0]] + [around(own[k], k) for k in range(1, GROUPS)]
    (shaped,) = call(shape_kernel, [(ROWS, COLS)], 2)(kappa, state)
    shaped, own[1] = lax.optimization_barrier((shaped, own[1]))
    other_shaped = across(shaped)
    other = call(pack_kernel, [(8, PIECE)] * 4, 1)(got)
    other = [other[0]] + [around(other[k], k) for k in range(1, GROUPS)]
    pieces = (*own, *other)
    edges = (EDGE, EDGES)
    source, near, far = call(
        scatter_kernel,
        [(VARS, ROWS, WIDE), edges, edges],
        9,
        scratch=[pltpu.VMEM((2 * VARS * ROWS, WIDE), jnp.float32)],
    )(obs_cell.reshape(1, OBS), *pieces)
    far, other_shaped = lax.optimization_barrier((far, other_shaped))
    far = beside(far, tiles, False)
    shaped, other_shaped, _ = lax.optimization_barrier((shaped, other_shaped, source))
    mixed = call(share_kernel, [(ROWS, COLS)] * 4, 3, smem=1)(mix, shaped, other_shaped)
    near, first = lax.optimization_barrier((near, mixed[0]))
    near = beside(near, tiles, True)
    mixed = [first] + [around(mixed[k], k) for k in range(1, GROUPS)]
    (far,) = call(far_kernel, [edges], 1, flops=1_000_000_000)(far)
    field = (VARS, TALL, WIDE)
    parts = call(
        main_kernel,
        [(8, 4 * BLOCK + SIDE)] * 4,
        12,
        smem=1,
        scratch=[pltpu.VMEM(field, jnp.float32)] * 5 + [pltpu.VMEM((TALL, WIDE), jnp.float32)],
    )(mix, source, near, far, *pieces)
    parts = [parts[0]] + [around(parts[k], k) for k in range(1, GROUPS)]
    adjoint, grad = call(join_kernel, [(ROWS, COLS)] * 2, 9)(*parts, *mixed, state)
    return adjoint[None], grad[None]


def solution(mesh):
    return jax.shard_map(
        functools.partial(per_device, mesh.shape["tile"]),
        mesh=mesh,
        in_specs=(P("var", "tile", None), P("var", "tile", None), P(), P("tile"), P("var", "tile")),
        out_specs=(P("var", "tile", None), P("var", "tile", None)),
        check_vma=False,
    )
```

```python
import functools

import jax
import jax.numpy as jnp
from jax import lax
from jax.experimental import pallas as pl
from jax.experimental.pallas import tpu as pltpu
from jax.sharding import PartitionSpec as P

ITERS = 4
THETA = 4.025
DELTA = 3.975
VMEM = pl.BlockSpec(memory_space=pltpu.VMEM)
SMEM = pl.BlockSpec(memory_space=pltpu.SMEM)

ROWS, COLS, VARS, GROUPS = 16, 2048, 8, 4
BLOCK = COLS // GROUPS
SIDE = 128
WIDE = BLOCK + SIDE
EDGE = 8
TALL = ROWS + 2 * EDGE
OBS = 4096
OBS_ROWS = OBS // BLOCK
EXTRA = ROWS // 8 * COLS
MIB = 1024 * 1024
SLIM = 16
P_OBS = 2 * BLOCK
P_STATE = P_OBS + BLOCK
P_SIDE = P_STATE + SIDE
PIECE = P_SIDE + SIDE
E_SOURCE = VARS * BLOCK
E_SIDE = 2 * VARS * BLOCK
E_STATE = E_SIDE + 2 * SIDE
EDGES = E_STATE + BLOCK


def group_place():
    var = lax.axis_index("var")
    return var // 2, lax.rem(var, 2)


def pack_side(packed, side, index):
    lane = lax.broadcasted_iota(jnp.int32, (8, SIDE), 1)
    here = (lane >= SLIM * index) & (lane < SLIM * index + SLIM)
    return jnp.where(here, pltpu.roll(side, lax.rem(SLIM * index + SLIM // 2, SIDE), 1), packed)


def unpack_side(packed, index):
    return pltpu.roll(packed, lax.rem(2 * SIDE - SLIM // 2 - SLIM * index, SIDE), 1)


def lanes_at(start, size):
    return pl.ds(pl.multiple_of(start, SIDE), size)


def ahead(y, k):
    return lax.rem(y + k, GROUPS)


def behind(y, k):
    return lax.rem(y - k + GROUPS, GROUPS)


def window(ref, block, row):
    start = row * COLS // 8
    main = ref[:, pl.ds(pl.multiple_of(start + block * BLOCK, BLOCK), BLOCK)]
    after = jnp.minimum(block + 1, GROUPS - 1) * BLOCK
    before = jnp.maximum(block * BLOCK - SIDE, 0)
    right = ref[:, pl.ds(pl.multiple_of(start + after, SIDE), SIDE)]
    left = ref[:, pl.ds(pl.multiple_of(start + before, SIDE), SIDE)]
    lane = lax.broadcasted_iota(jnp.int32, (8, SIDE), 1)
    return main, jnp.where(lane < SIDE // 2, right, left)


def first_kernel(kappa_hbm, obs_hbm, state_hbm, sent_ref, kappa_ref, obs_ref, state_ref, sems):
    edges = [(state_hbm.at[r : r + 1, :], state_ref.at[i : i + 1, :]) for i, r in enumerate((0, ROWS - 1))]
    pairs = [(kappa_hbm, kappa_ref), (obs_hbm, obs_ref)] + edges
    copies = [pltpu.make_async_copy(src, dst, sems.at[i]) for i, (src, dst) in enumerate(pairs)]
    for one in copies:
        one.start()
    for one in copies:
        one.wait()
    for r in range(0, ROWS, 8):
        sent_ref[:, r // 8 * COLS : (r // 8 + 1) * COLS] = kappa_ref[r : r + 8]
    for i in range(OBS_ROWS):
        sent_ref[i : i + 1, EXTRA : EXTRA + BLOCK] = obs_ref[:, i * BLOCK : (i + 1) * BLOCK]
    for e in range(2):
        for block in range(GROUPS):
            for i in range(BLOCK // SIDE):
                to, at = e * (BLOCK // SIDE) + i, EXTRA + BLOCK + block * SIDE
                col = block * BLOCK + i * SIDE
                sent_ref[to : to + 1, at : at + SIDE] = state_ref[e : e + 1, col : col + SIDE]


def shape_kernel(kappa_ref, state_ref, shaped_ref):
    u = state_ref[...]
    row = lax.broadcasted_iota(jnp.int32, (ROWS, COLS), 0)
    lane = lax.broadcasted_iota(jnp.int32, (ROWS, COLS), 1)
    beside = jnp.where(row > 0, pltpu.roll(u, 1, 0), 0.0) + jnp.where(row < ROWS - 1, pltpu.roll(u, ROWS - 1, 0), 0.0)
    beside = beside + jnp.where(lane > 0, pltpu.roll(u, 1, 1), 0.0)
    beside = beside + jnp.where(lane < COLS - 1, pltpu.roll(u, COLS - 1, 1), 0.0)
    shaped_ref[...] = (kappa_ref[...] + 4.0) * u - beside


def hold_kernel(sent_ref, held_ref):
    held_ref[...] = sent_ref[...]


def pack_kernel(ref, *outs):
    y, _ = group_place()
    for k in range(GROUPS):
        block = ahead(y, k)
        packed = jnp.zeros((8, SIDE), jnp.float32)
        for half in range(ROWS // 8):
            main, side = window(ref, block, half * 8)
            outs[k][:, half * BLOCK : (half + 1) * BLOCK] = main
            packed = pack_side(packed, side, half)
        outs[k][:, P_OBS:P_STATE] = ref[:, EXTRA : EXTRA + BLOCK]
        outs[k][:, P_STATE:P_SIDE] = ref[:, lanes_at(EXTRA + BLOCK + block * SIDE, SIDE)]
        outs[k][:, P_SIDE:] = packed


def scatter_kernel(cell_ref, *refs):
    y, z = group_place()
    core = lax.rem(lax.axis_index("tile"), 2)
    pieces, (source_ref, near_ref, far_ref, acc) = (refs[:GROUPS], refs[GROUPS : 2 * GROUPS]), refs[2 * GROUPS :]
    acc[...] = jnp.zeros_like(acc)
    rows = lax.broadcasted_iota(jnp.int32, (ROWS, BLOCK), 0)
    lanes = lax.broadcasted_iota(jnp.int32, (WIDE, BLOCK), 0)
    half = SIDE // 2
    for i in range(OBS_ROWS):
        cell = cell_ref[:, i * BLOCK : (i + 1) * BLOCK]
        row = lax.shift_right_logical(cell, 11)
        col = jnp.bitwise_and(cell, COLS - 1) - y * BLOCK
        place = jnp.where(
            (col >= 0) & (col < BLOCK + half), col, jnp.where((col >= -half) & (col < 0), col + WIDE, -1)
        )
        hit_row = rows == row
        hit_col = jnp.where(lanes == place, 1.0, 0.0).astype(jnp.bfloat16)
        highs, lows = [], []
        for k in range(GROUPS):
            for slot in range(2):
                value = pieces[slot][k][i : i + 1, P_OBS:P_STATE]
                high = value.astype(jnp.bfloat16).astype(jnp.float32)
                low = value - high
                highs.append(jnp.where(hit_row, high, 0.0).astype(jnp.bfloat16))
                lows.append(jnp.where(hit_row, low, 0.0).astype(jnp.bfloat16))
        values = jnp.concatenate(highs + lows, axis=0)
        acc[...] += lax.dot_general(
            values, hit_col, (((1,), (1,)), ((), ())), preferred_element_type=jnp.float32
        )
    count = VARS * ROWS
    for k in range(GROUPS):
        for slot in range(2):
            at = (k * 2 + slot) * ROWS
            total = acc[at : at + ROWS] + acc[count + at : count + at + ROWS]
            var = 2 * behind(y, k) + lax.rem(z + slot, 2)
            source_ref[var] = total
    for ref, last in ((near_ref, 1 - core), (far_ref, core)):
        packed_kappa = packed_source = jnp.zeros((8, SIDE), jnp.float32)
        for k in range(GROUPS):
            for slot in range(2):
                var = 2 * behind(y, k) + lax.rem(z + slot, 2)
                kappa = pieces[slot][k][:, lanes_at(last * BLOCK, BLOCK)]
                ref[:, lanes_at(var * BLOCK, BLOCK)] = kappa
                side = unpack_side(pieces[slot][k][:, P_SIDE:], last)
                packed_kappa = pack_side(packed_kappa, side, var)
                total = source_ref[var, pl.ds(pl.multiple_of(EDGE * last, EDGE), EDGE)]
                ref[:, lanes_at(E_SOURCE + var * BLOCK, BLOCK)] = total[:, :BLOCK]
                packed_source = pack_side(packed_source, total[:, BLOCK:], var)
        ref[:, E_SIDE : E_SIDE + SIDE] = packed_kappa
        ref[:, E_SIDE + SIDE : E_STATE] = packed_source
    sub = lax.broadcasted_iota(jnp.int32, (VARS, SIDE), 0)
    for i in range(BLOCK // SIDE):
        held = []
        for e in range(2):
            row = e * (BLOCK // SIDE) + i
            rows = jnp.zeros((VARS, SIDE), jnp.float32)
            for k in range(GROUPS):
                for slot in range(2):
                    var = 2 * behind(y, k) + lax.rem(z + slot, 2)
                    rows = jnp.where(sub == var, pieces[slot][k][row : row + 1, P_STATE:P_SIDE], rows)
            held.append(rows)
        here = slice(E_STATE + i * SIDE, E_STATE + (i + 1) * SIDE)
        near_ref[:, here] = jnp.where(core == 0, held[1], held[0])
        far_ref[:, here] = jnp.where(core == 0, held[0], held[1])


def share_kernel(mix_ref, own_ref, other_ref, *outs):
    y, z = group_place()
    for k in range(GROUPS):
        v = 2 * ahead(y, k) + z
        one, two = mix_ref[v, 2 * y + z], mix_ref[v, 2 * y + 1 - z]
        for r in range(0, ROWS, 8):
            outs[k][r : r + 8] = one * own_ref[r : r + 8] + two * other_ref[r : r + 8]


def shape_rows(u):
    return pltpu.roll(u, 1, 0) + pltpu.roll(u, TALL - 1, 0) + pltpu.roll(u, 1, 1) + pltpu.roll(u, WIDE - 1, 1)


def far_kernel(far_ref, out_ref):
    out_ref[...] = far_ref[...]


def main_kernel(mix_ref, source_ref, near_ref, far_ref, *refs):
    pieces, outs = (refs[:GROUPS], refs[GROUPS : 2 * GROUPS]), refs[2 * GROUPS : 3 * GROUPS]
    adj, kp, res, dirn, tmp, mask_ref = refs[3 * GROUPS :]
    y, z = group_place()
    tile = lax.axis_index("tile")
    row = lax.broadcasted_iota(jnp.int32, (TALL, WIDE), 0)
    lane = lax.broadcasted_iota(jnp.int32, (TALL, WIDE), 1)
    row = jnp.where(row < ROWS + EDGE, row, row - TALL) + tile * ROWS
    lane = jnp.where(lane < BLOCK + SIDE // 2, lane, lane - WIDE) + y * BLOCK
    inside = (row >= 0) & (row < ROWS * lax.axis_size("tile")) & (lane >= 0) & (lane < COLS)
    mask_ref[...] = jnp.where(inside, 1.0, 0.0)
    for k in range(GROUPS):
        for slot in range(2):
            var = 2 * behind(y, k) + lax.rem(z + slot, 2)
            for half in range(ROWS // 8):
                rows, piece = slice(half * 8, half * 8 + 8), pieces[slot][k]
                mask = mask_ref[rows]
                kappa = piece[:, half * BLOCK : (half + 1) * BLOCK]
                kp[var, rows, :BLOCK] = (kappa + 4.0) * mask[:, :BLOCK]
                kp[var, rows, BLOCK:] = (unpack_side(piece[:, P_SIDE:], half) + 4.0) * mask[:, BLOCK:]
    core = lax.rem(tile, 2)

    def start(var, rows, cols, part):
        res[var, rows, cols] = part
        part = part * (1.0 / THETA)
        dirn[var, rows, cols] = part
        adj[var, rows, cols] = part

    main, edge = slice(0, BLOCK), slice(BLOCK, WIDE)
    for at, ref in ((ROWS + EDGE * core, near_ref), (ROWS + EDGE * (1 - core), far_ref)):
        rows = pl.ds(pl.multiple_of(at, EDGE), EDGE)
        mask = mask_ref[rows]
        for var in range(VARS):
            kp[var, rows, main] = (ref[:, var * BLOCK : (var + 1) * BLOCK] + 4.0) * mask[:, main]
            kp[var, rows, edge] = (unpack_side(ref[:, E_SIDE : E_SIDE + SIDE], var) + 4.0) * mask[:, edge]
            at = E_SOURCE + var * BLOCK
            start(var, rows, main, ref[:, at : at + BLOCK] * mask[:, main])
            start(var, rows, edge, unpack_side(ref[:, E_SIDE + SIDE : E_STATE], var) * mask[:, edge])
    for var in range(VARS):
        start(var, slice(0, ROWS), slice(0, WIDE), source_ref[var] * mask_ref[:ROWS])

    def shape(src, var):
        u = src[var]
        beside = shape_rows(u)
        side = beside[:ROWS, BLOCK:] * mask_ref[:ROWS, BLOCK:]
        own = jnp.concatenate([beside[:ROWS, :BLOCK], side], axis=1)
        return kp[var] * u - jnp.concatenate([own, beside[ROWS:] * mask_ref[ROWS:]], axis=0)

    def couple(ref):
        for r in range(0, TALL, 8):
            fields = [ref[w, r : r + 8] for w in range(VARS)]
            for v in range(VARS):
                total = mix_ref[v, 0] * fields[0]
                for w in range(1, VARS):
                    total = total + mix_ref[v, w] * fields[w]
                ref[v, r : r + 8] = total

    sigma = THETA / DELTA
    rho = 1.0 / sigma
    for _ in range(ITERS - 1):
        rho_new = 1.0 / (2.0 * sigma - rho)
        c1, c2 = rho_new * rho, 2.0 * rho_new / DELTA
        rho = rho_new

        for var in range(VARS):
            tmp[var] = shape(dirn, var)
        couple(tmp)

        for var in range(VARS):
            r = res[var] - shape(tmp, var)
            res[var] = r
            d = c1 * dirn[var] + c2 * r
            dirn[var] = d
            adj[var] = adj[var] + d

    for var in range(VARS):
        u = adj[var]
        tmp[var, :ROWS, :BLOCK] = kp[var, :ROWS, :BLOCK] * u[:ROWS, :BLOCK] - shape_rows(u)[:ROWS, :BLOCK]
    for k, out in enumerate(outs):
        v = 2 * ahead(y, k) + z
        for c in range(0, BLOCK, 128):
            cols = slice(c, c + 128)
            here = slice(E_STATE + c, E_STATE + c + 128)
            near = mix_ref[v, 0] * near_ref[0:1, here]
            far = mix_ref[v, 0] * far_ref[0:1, here]
            for w in range(1, VARS):
                near = near + mix_ref[v, w] * near_ref[w : w + 1, here]
                far = far + mix_ref[v, w] * far_ref[w : w + 1, here]
            i = c // SIDE
            out[i : i + 1, 4 * BLOCK :] = jnp.where(core == 0, far, near)
            out[4 + i : 5 + i, 4 * BLOCK :] = jnp.where(core == 0, near, far)
            for half in range(ROWS // 8):
                rows = slice(half * 8, half * 8 + 8)
                total = mix_ref[v, 0] * tmp[0, rows, cols]
                for w in range(1, VARS):
                    total = total + mix_ref[v, w] * tmp[w, rows, cols]
                out[:, half * BLOCK + c : half * BLOCK + c + 128] = adj[v, rows, cols]
                out[:, (2 + half) * BLOCK + c : (2 + half) * BLOCK + c + 128] = total


def join_kernel(p0, p1, p2, p3, m0, m1, m2, m3, state_ref, adjoint_ref, grad_ref):
    y, _ = group_place()
    row = lax.broadcasted_iota(jnp.int32, (8, SIDE), 0)
    for k, part in enumerate((p0, p1, p2, p3)):
        for half in range(ROWS // 8):
            rows = slice(half * 8, half * 8 + 8)
            for i in range(BLOCK // SIDE):
                cols = lanes_at(behind(y, k) * BLOCK + i * SIDE, SIDE)
                mixed = (m0[rows, cols] + m1[rows, cols]) + (m2[rows, cols] + m3[rows, cols])
                edge = 4 * half + i
                mixed = mixed - jnp.where(row == 7 * half, part[edge : edge + 1, 4 * BLOCK :], 0.0)
                at = half * BLOCK + i * SIDE
                adjoint = part[:, at : at + SIDE]
                at += 2 * BLOCK
                adjoint_ref[rows, cols] = adjoint
                grad_ref[rows, cols] = -(part[:, at : at + SIDE] * state_ref[rows, cols] + adjoint * mixed)


def call(kernel, outs, n_in, smem=0, scratch=(), flops=1000, size=100000, hbm=0, limit=32):
    shapes = [jax.ShapeDtypeStruct(s, jnp.float32) for s in outs]
    return pl.pallas_call(
        kernel,
        out_shape=shapes,
        in_specs=[SMEM] * smem + [pl.BlockSpec(memory_space=pl.ANY)] * hbm + [VMEM] * (n_in - smem - hbm),
        out_specs=[VMEM] * len(shapes),
        scratch_shapes=list(scratch),
        compiler_params=pltpu.CompilerParams(vmem_limit_bytes=limit * MIB),
        cost_estimate=pl.CostEstimate(flops=flops, bytes_accessed=size, transcendentals=0),
    )


def across(x):
    return lax.ppermute(x, "var", [(i, i ^ 1) for i in range(VARS)])


def around(x, k):
    return lax.ppermute(x, "var", [(i, (i // 2 + k) % GROUPS * 2 + i % 2) for i in range(VARS)])


def beside(x, tiles, near):
    pairs = []
    for i in range(0 if near else 1, tiles - 1, 2):
        for v in range(VARS):
            one, two = i * VARS + v, (i + 1) * VARS + (v ^ 1 if i % 8 == 7 else v)
            pairs += [(one, two), (two, one)]
    return lax.ppermute(x, ("tile", "var"), pairs)


def per_device(tiles, range_sq, state_field, coupling, obs_cell, obs_value):
    mixing = jnp.eye(VARS, dtype=jnp.float32) + coupling
    mix = jnp.einsum("uv,uw->vw", mixing, mixing, precision=lax.Precision.HIGHEST) * (1.0 / 64.0)
    kappa, state = range_sq[0], state_field[0]
    (sent,) = call(
        first_kernel,
        [(8, EXTRA + 2 * BLOCK)],
        3,
        hbm=3,
        limit=56,
        scratch=[pltpu.VMEM((ROWS, COLS), jnp.float32), pltpu.VMEM((1, OBS), jnp.float32)]
        + [pltpu.VMEM((2, COLS), jnp.float32), pltpu.SemaphoreType.DMA((4,))],
    )(kappa, obs_value, state)
    got = across(sent)
    (sent,) = call(hold_kernel, [(8, EXTRA + 2 * BLOCK)], 1)(sent)
    own = call(pack_kernel, [(8, PIECE)] * 4, 1)(sent)
    own = [own[0]] + [around(own[k], k) for k in range(1, GROUPS)]
    (shaped,) = call(shape_kernel, [(ROWS, COLS)], 2)(kappa, state)
    shaped, own[1] = lax.optimization_barrier((shaped, own[1]))
    other_shaped = across(shaped)
    other = call(pack_kernel, [(8, PIECE)] * 4, 1)(got)
    other = [other[0]] + [around(other[k], k) for k in range(1, GROUPS)]
    pieces = (*own, *other)
    edges = (EDGE, EDGES)
    source, near, far = call(
        scatter_kernel,
        [(VARS, ROWS, WIDE), edges, edges],
        9,
        scratch=[pltpu.VMEM((2 * VARS * ROWS, WIDE), jnp.float32)],
    )(obs_cell.reshape(1, OBS), *pieces)
    far, other_shaped = lax.optimization_barrier((far, other_shaped))
    far = beside(far, tiles, False)
    shaped, other_shaped, _ = lax.optimization_barrier((shaped, other_shaped, source))
    mixed = call(share_kernel, [(ROWS, COLS)] * 4, 3, smem=1)(mix, shaped, other_shaped)
    near, first = lax.optimization_barrier((near, mixed[0]))
    near = beside(near, tiles, True)
    mixed = [first] + [around(mixed[k], k) for k in range(1, GROUPS)]
    (far,) = call(far_kernel, [edges], 1, flops=1_000_000_000)(far)
    field = (VARS, TALL, WIDE)
    parts = call(
        main_kernel,
        [(8, 4 * BLOCK + SIDE)] * 4,
        12,
        smem=1,
        scratch=[pltpu.VMEM(field, jnp.float32)] * 5 + [pltpu.VMEM((TALL, WIDE), jnp.float32)],
    )(mix, source, near, far, *pieces)
    parts = [parts[0]] + [around(parts[k], k) for k in range(1, GROUPS)]
    adjoint, grad = call(join_kernel, [(ROWS, COLS)] * 2, 9)(*parts, *mixed, state)
    return adjoint[None], grad[None]


def solution(mesh):
    return jax.shard_map(
        functools.partial(per_device, mesh.shape["tile"]),
        mesh=mesh,
        in_specs=(P("var", "tile", None), P("var", "tile", None), P(), P("tile"), P("var", "tile")),
        out_specs=(P("var", "tile", None), P("var", "tile", None)),
        check_vma=False,
    )
```
